128 devices in a mesh: dev: 128 (over y, x, z, core).
Axes of the slice: x: 4, y: 4, z: 4, core: 2. Of those that a mesh axis runs over, the one named last changes fastest.
Arguments:
- conductivity: float32 [512, 3, 2048], P('dev'), may hold values from 0.05 to 1
- block_ids: int32 [1024, 16], P('dev'), may hold values from 0 to 511, as said below
- weights: int32 [1024, 8], P('dev'), may hold values from 1 to 7
- source: float32 [1024, 3, 8, 16, 128], P('dev'), may hold values from -6 to 6
- cotangent: float32 [1024, 3, 8, 16, 128], P('dev'), may hold values from -6 to 6
Outputs:
- fields: float32 [1024, 3, 8, 16, 128], P('dev')
- gradient: float32 [512, 3, 2048], P('dev')
The draws below stay inside these ranges and needn't reach their ends.
Inputs may be any that keep to these rules, and one draw needn't show every extreme that they name: `block_ids`: the 128 entries of the meshes of one device (an aligned block of 8 rows) name blocks of all owners, each owner exactly once, the owner of a block being its id // 4.
All inputs are finite; a program needn't handle non-finite values.
Results may differ from the reference program's by a relative error of at most 0.00002.
Values sent between devices are 32-bit elements; how exact they have to be, the bound alone decides.
A program may use at most 128 MiB of HBM per device.

```python
import math
import jax
import jax.numpy as jnp
from jax import lax

MX = 8
MY = 16
MZ = 128
STEPS = 10
BLK_DEV = 4
MESH_DEV = 8
BC = 2048
NBLK = 512
MESHES = 1024
N_DEV = 128


def draw_block_ids(key, part):
    entry_count = MESH_DEV * 2 * MX

    def per_device(device_number):
        device_key = jax.random.fold_in(key, device_number)
        owners = jax.random.permutation(jax.random.fold_in(device_key, 11), N_DEV)[:entry_count]
        local_rows = jax.random.randint(jax.random.fold_in(device_key, 23), (entry_count,), 0, BLK_DEV)
        return (owners * BLK_DEV + local_rows).reshape(MESH_DEV, 2 * MX)
    table = jax.vmap(per_device)(jnp.arange(N_DEV))
    return table.reshape(MESH_DEV * N_DEV, 2 * MX).astype(jnp.int32)


def plant(array, rng, low, largest):
    place = [jax.random.randint(jax.random.fold_in(rng, axis), (), 0, length) for axis, length in enumerate(array.shape)]
    longest = array.shape.index(max(array.shape))
    next_to = place[:longest] + [(place[longest] + 1) % array.shape[longest]] + place[longest + 1:]
    return array.at[tuple(place)].set(low).at[tuple(next_to)].set(largest)


def level_of(rng, shape, split, least, top_value):
    level = 1.0
    for axis_at, parts in split:
        heights = jax.random.uniform(jax.random.fold_in(jax.random.fold_in(rng, 6), axis_at), (parts,), jnp.float32, least / len(split), top_value / len(split))
        level = level * jnp.repeat(jnp.exp(heights), shape[axis_at] // parts).reshape((-1,) + (1,) * (len(shape) - 1 - axis_at))
    return level


def normal_values(stream_key, shape, deviation, limit, pieces=(), held_as=jnp.bfloat16):
    factor_of = level_of(stream_key, shape, pieces, -0.22, 0.18) if pieces else 1.0
    array = jax.random.normal(stream_key, shape, jnp.float32) * deviation * factor_of
    return jnp.minimum(jnp.maximum(array, -limit), limit).astype(held_as)


def setup_inputs(seed: int = 0) -> dict:
    streams_of = jax.random.split(jax.random.key(seed), 6)
    return {
        "conductivity": jnp.clip(jnp.exp(math.log(1.0) - 2.9957323 * jax.random.uniform(streams_of[0], (NBLK, 3, BC), jnp.float32) ** level_of(streams_of[0], (NBLK, 3, BC), ((0, 128),), -0.2, 0.2)), 0.05, 1.0),
        "block_ids": draw_block_ids(jax.random.fold_in(streams_of[5], 71), 0),
        "weights": plant(jax.random.randint(streams_of[2], (MESHES, MX), 1, 8), jax.random.fold_in(streams_of[2], 1), 1, 7).astype(jnp.int32),
        "source": normal_values(streams_of[3], (MESHES, 3, MX, MY, MZ), 1.0, 6.0, ((0, 128),), jnp.float32),
        "cotangent": normal_values(streams_of[4], (MESHES, 3, MX, MY, MZ), 1.0, 6.0, ((0, 128),), jnp.float32),
    }


time_step = 0.5

def difference(values, direction, forward):
    length = values.shape[direction]
    zero_plane = jnp.zeros_like(lax.slice_in_dim(values, 0, 1, axis=direction))
    if forward:
        later = jnp.concatenate([lax.slice_in_dim(values, 1, length, axis=direction), zero_plane], axis=direction)
        return later - values
    earlier = jnp.concatenate([zero_plane, lax.slice_in_dim(values, 0, length - 1, axis=direction)], axis=direction)
    return values - earlier

def curl_of(vector, forward):
    first = difference(vector[2], 1, forward) - difference(vector[1], 2, forward)
    second = difference(vector[0], 2, forward) - difference(vector[2], 0, forward)
    third = difference(vector[1], 0, forward) - difference(vector[0], 1, forward)
    return jnp.stack([first, second, third])

def evolve(damping, initial):

    def leapfrog(state_pair, unused_item):
        electric, magnetic = state_pair
        magnetic = magnetic - time_step * curl_of(electric, True)
        electric = electric + time_step * (curl_of(magnetic, False) - damping * electric)
        return ((electric, magnetic), None)
    final_pair, unused_out = lax.scan(leapfrog, (initial, jnp.zeros_like(initial)), None, length=STEPS)
    return final_pair[0]

def mesh_field(picked, mesh_weights, initial):
    fraction = mesh_weights.astype(jnp.float32) / 8.0
    near_part = picked[:MX]
    far_part = picked[MX:]
    damping = fraction[:, None, None] * near_part + (1.0 - fraction)[:, None, None] * far_part
    damping = jnp.swapaxes(damping, 0, 1).reshape(3, MX, MY, MZ)
    return evolve(damping, initial)

def reference(conductivity, block_ids, weights, source, cotangent):

    def single_mesh(mesh_items):
        mesh_ids, mesh_weights, mesh_source, mesh_cotangent = mesh_items
        picked = conductivity[mesh_ids]
        electric, pullback = jax.vjp(lambda blocks_in: mesh_field(blocks_in, mesh_weights, mesh_source), picked)
        mesh_grads, = pullback(mesh_cotangent)
        return (electric, mesh_grads)
    fields, grads = lax.map(single_mesh, (block_ids, weights, source, cotangent))
    flat_ids = block_ids.reshape(-1).astype(jnp.int32)
    gradient = jnp.zeros_like(conductivity).at[flat_ids].add(grads.reshape(flat_ids.shape[0], 3, MY * MZ))
    return (fields, gradient)
```

```python
import jax, jax.numpy as jnp
from jax import lax
from jax.experimental import pallas as pl
from jax.experimental.pallas import tpu as pltpu
from jax.sharding import PartitionSpec as P

MX, MY, MZ, STEPS = 8, 16, 128, 10
HALF = STEPS // 2


def sweep(src, dst, mag, decay, masks, x, visit):
    first, last = masks
    olds = [[s(c, x, 0) for c in range(3)] for s in src]
    befores = [None] * len(src)
    for y in range(MY):
        keep = [decay[c, x, y] for c in range(3)]
        for k in range(len(src)):
            ex, ey, ez = olds[k]
            exz = jnp.where(last, 0.0, pltpu.roll(ex, MZ - 1, 1))
            eyz = jnp.where(last, 0.0, pltpu.roll(ey, MZ - 1, 1))
            eyx, ezx = src[k](1, x + 1, y), src[k](2, x + 1, y)
            h = mag[k]
            if y + 1 < MY:
                nexts = [src[k](c, x, y + 1) for c in range(3)]
                gx = h[0, x + 1, y] + ((nexts[2] - eyz) + (ey - ez))
                gz = h[2, x + 1, y] + ((eyx - nexts[0]) + (ex - ey))
            else:
                nexts = None
                gx = h[0, x + 1, y] + ((ey - ez) - eyz)
                gz = h[2, x + 1, y] + (eyx + (ex - ey))
            gy = h[1, x + 1, y] + ((exz - ezx) + (ez - ex))
            h[0, x + 1, y] = gx
            h[1, x + 1, y] = gy
            h[2, x + 1, y] = gz
            gxz = jnp.where(first, 0.0, pltpu.roll(gx, 1, 1))
            gyz = jnp.where(first, 0.0, pltpu.roll(gy, 1, 1))
            gyx, gzx = h[1, x, y], h[2, x, y]
            if y > 0:
                bx, bz = befores[k]
                cx = (gz - gy) + (gyz - bz)
                cz = (gy - gx) + (bx - gyx)
            else:
                cx = (gz - gy) + gyz
                cz = (gy - gx) - gyx
            cy = (gx - gz) + (gzx - gxz)
            new = [keep[c] * olds[k][c] - 0.25 * v for c, v in enumerate((cx, cy, cz))]
            visit(k, y, olds[k], new)
            befores[k] = (gx, gz)
            olds[k] = nexts


def compute_kernel(entry, weight, near, source, cotangent, fields, slots, hist, mag, decay, grad):
    lane = lax.broadcasted_iota(jnp.int32, (8, MZ), 1)
    masks = (lane == 0, lane == MZ - 1)
    zero = jnp.zeros((MY, 8, MZ), jnp.float32)
    for k in range(2):
        for c in range(3):
            mag[k, c, 0] = zero
            for n in range(HALF + 1):
                hist[k, n, c, MX] = zero

            def clear(x, carry):
                mag[k, c, x + 1] = zero
                return carry
            lax.fori_loop(0, MX, clear, 0)

    def stage(i, carry):
        c, x = i // MX, i % MX
        for y in range(MY):
            row = pl.ds(i * MY + y, 8, stride=3 * MX * MY)
            hist[0, 0, c, x, y] = source[row, :]
            hist[1, 0, c, x, y] = cotangent[row, :]
        return carry
    lax.fori_loop(0, 3 * MX, stage, 0)

    flat_decay = decay.reshape(3 * MX * MY * 8, MZ)
    flat_grad = grad.reshape(3 * MX * MY * 8, MZ)

    def blend(i, carry):
        m, x = i // MX, i % MX
        f = weight[m, x].astype(jnp.float32) * 0.125
        for c in range(3):
            close = near[c, entry[c, m * 2 * MX + x]]
            far = near[c, entry[c, m * 2 * MX + MX + x]]
            flat_decay[pl.ds((c * MX + x) * (MY * 8) + m, MY, stride=8), :] = 1.0 - 0.5 * (f * close + (1.0 - f) * far)
        return carry
    lax.fori_loop(0, 8 * MX, blend, 0)

    def early(n, carry):
        def plane(x, carry):
            src = [lambda c, xx, y, k=k: hist[k, n, c, xx, y] for k in range(2)]

            def visit(k, y, old, new):
                for c in range(3):
                    hist[k, n + 1, c, x, y] = new[c]
            sweep(src, None, [mag.at[0], mag.at[1]], decay, masks, x, visit)
            return carry
        return lax.fori_loop(0, MX, plane, carry)
    lax.fori_loop(0, HALF, early, 0)

    def late(n, carry):
        def plane(x, carry):
            src = [lambda c, xx, y, k=k: hist[k, HALF, c, xx, y] for k in range(2)]
            part = {}

            def visit(k, y, old, new):
                terms = [old[c] * hist[1 - k, STEPS - 1 - n, c, x, y] for c in range(3)]
                if k == 0:
                    part[y] = terms
                else:
                    for c in range(3):
                        grad[c, x, y] = (grad[c, x, y] if n is not HALF else 0.0) + (part[y][c] + terms[c])
                for c in range(3):
                    hist[k, HALF, c, x, y] = new[c]
            sweep(src, None, [mag.at[0], mag.at[1]], decay, masks, x, visit)
            return carry
        return lax.fori_loop(0, MX, plane, carry)
    late(HALF, 0)
    lax.fori_loop(HALF + 1, STEPS - 1, late, 0)

    def final(x, carry):
        src = [lambda c, xx, y: hist[0, HALF, c, xx, y]]

        def visit(k, y, old, new):
            for c in range(3):
                fields[pl.ds((c * MX + x) * MY + y, 8, stride=3 * MX * MY), :] = new[c]
                grad[c, x, y] = grad[c, x, y] + (old[c] * hist[1, 0, c, x, y] + hist[1, HALF, c, x, y] * hist[0, 0, c, x, y])
        sweep(src, None, [mag.at[0]], decay, masks, x, visit)
        return carry
    lax.fori_loop(0, MX, final, 0)

    def spread(i, carry):
        m, x = i // MX, i % MX
        f = weight[m, x].astype(jnp.float32) * 0.125
        for c in range(3):
            g = flat_grad[pl.ds((c * MX + x) * (MY * 8) + m, MY, stride=8), :]
            slots[c, entry[c, m * 2 * MX + x]] = (-0.5 * f) * g
            slots[c, entry[c, m * 2 * MX + MX + x]] = (-0.5 * (1.0 - f)) * g
        return carry
    lax.fori_loop(0, 8 * MX, spread, 0)


def compute(entry, weight, near, source, cotangent):
    vmem = pl.BlockSpec(memory_space=pltpu.VMEM)
    smem = pl.BlockSpec(memory_space=pltpu.SMEM)
    f32 = jnp.float32
    return pl.pallas_call(
        compute_kernel,
        out_shape=(jax.ShapeDtypeStruct((8 * 3 * MX * MY, MZ), f32), jax.ShapeDtypeStruct((3, 128, MY, MZ), f32)),
        in_specs=[smem, smem, vmem, vmem, vmem],
        out_specs=(vmem, vmem),
        scratch_shapes=[
            pltpu.VMEM((2, HALF + 1, 3, MX + 1, MY, 8, MZ), f32),
            pltpu.VMEM((2, 3, MX + 1, MY, 8, MZ), f32),
            pltpu.VMEM((3, MX, MY, 8, MZ), f32),
            pltpu.VMEM((3, MX, MY, 8, MZ), f32),
        ],
        compiler_params=pltpu.CompilerParams(vmem_limit_bytes=60 * 2**20),
    )(entry, weight, near, source, cotangent)


def local(conductivity, block_ids, weights, source, cotangent):
    count = lax.axis_size("dev")
    blocks_here = conductivity.shape[0]
    flat = block_ids.reshape(-1)
    owner, index = flat // blocks_here, flat % blocks_here
    hit = owner[:, None] == jnp.arange(count, dtype=jnp.int32)[None, :]
    wanted = jnp.sum(jnp.where(hit, index[:, None], 0), axis=0).astype(jnp.int32)
    asked = lax.all_to_all(wanted.reshape(count, 1), "dev", split_axis=0, concat_axis=0, tiled=True).reshape(count)
    blocks = conductivity.reshape(blocks_here, 3, MY, MZ)
    pick = asked[:, None, None, None]
    outgoing = jnp.where(
        pick < 2, jnp.where(pick == 0, blocks[:1], blocks[1:2]), jnp.where(pick == 2, blocks[2:3], blocks[3:])
    )
    arrived = lax.all_to_all(outgoing, "dev", split_axis=0, concat_axis=0, tiled=True)
    fields, slots = compute(
        jnp.stack([owner] * 3), weights, arrived.transpose(1, 0, 2, 3), source.reshape(-1, MZ), cotangent.reshape(-1, MZ)
    )
    back = lax.all_to_all(slots.transpose(1, 0, 2, 3), "dev", split_axis=0, concat_axis=0, tiled=True)
    gradient = jnp.stack(
        [jnp.sum(jnp.where((asked == k)[:, None, None, None], back, 0.0), axis=0) for k in range(4)]
    )
    return fields.reshape(source.shape), gradient.reshape(conductivity.shape)


def solution(mesh):
    rows = P("dev")
    return jax.shard_map(
        local, mesh=mesh, in_specs=(rows,) * 5, out_specs=(rows, rows), check_vma=False
    )
```

```python
import jax, jax.numpy as jnp
from jax import lax
from jax.experimental import pallas as pl
from jax.experimental.pallas import tpu as pltpu
from jax.sharding import PartitionSpec as P

MX, MY, MZ, STEPS = 8, 16, 128, 10
HALF = STEPS // 2
MESH = pl.DeviceIdType.MESH
STRIDE = {"y": 32, "x": 8, "z": 2}
ORDERS = (("y", "x", "z"), ("x", "z", "y"), ("z", "y", "x"))
FAR = (2, 1, 3)


def place():
    me = lax.axis_index("dev")
    return me, {"y": me // 32, "x": (me // 8) % 4, "z": (me // 2) % 4}, me % 2


def shifted(me, at, dim, k):
    return me + ((at[dim] + k) % 4 - at[dim]) * STRIDE[dim]


def other_core(me, core, q):
    return me + (1 - 2 * core) * q


def column(me, at, core, dim, t, q):
    return other_core(shifted(me, at, dim, t), core, q)


def neighbours(me, at, core):
    out = [other_core(me, core, 1)]
    for dim in ("y", "x", "z"):
        for t in FAR:
            for q in (0, 1):
                out.append(column(me, at, core, dim, t, q))
    return out


def greet(me, at, core):
    barrier = pltpu.get_barrier_semaphore()
    near = neighbours(me, at, core)
    for other in near:
        pl.semaphore_signal(barrier, inc=1, device_id=(other,), device_id_type=MESH)
    pl.semaphore_wait(barrier, len(near))


def remote(src, dst, send, recv, device):
    return pltpu.make_async_remote_copy(
        src_ref=src, dst_ref=dst, send_sem=send, recv_sem=recv, device_id=(device,), device_id_type=MESH
    )


DIMS = ("y", "x", "z")
REACH = [(t, q) for t in (2, 1, 3, 0) for q in (1, 0) if (t, q) != (0, 0)]


def fetch_kernel(ids, model, arrived, asked, wish, gather, picked, asked_s, asked_v,
                 s_wish, r_wish, s_a1, r_a1, s_a2, r_a2, s_b, r_b, s_loc):
    me, at, core = place()
    pair = other_core(me, core, 1)
    lane = lax.broadcasted_iota(jnp.int32, (8, MZ), 1)

    def request(e, wanted):
        block = ids[e // 16, e % 16]
        return jnp.where(lane == (block >> 2), block & 3, wanted)
    wanted = lax.fori_loop(0, 128, request, jnp.zeros((8, MZ), jnp.int32))
    wish[...] = wanted
    for c, (a1, a2, b) in enumerate(ORDERS):
        asked_v[c, 0, 0] = wanted
        for k in range(4):
            gather[c][0][at[a1], k] = model[pl.ds(c * 64 + k, MY, stride=4), :]
    greet(me, at, core)
    started = []

    def go(copy):
        copy.start()
        started.append(copy)

    for k in FAR:
        for c, (a1, a2, b) in enumerate(ORDERS):
            own = gather[c][0].at[at[a1]]
            go(remote(own, own, s_a1.at[c, k], r_a1.at[c, k], shifted(me, at, a1, k)))
    for c, (a1, a2, b) in enumerate(ORDERS):
        for t, q in REACH:
            go(remote(wish, asked_v.at[c, t, q], s_wish.at[c, t, q], r_wish.at[c, t, q], column(me, at, core, b, t, q)))
    for j in (0, 1, 3, 2):
        for c, (a1, a2, b) in enumerate(ORDERS):
            at_j = (at[a1] + 4 - j) % 4
            slot = gather[c][0].at[at_j]
            if j:
                remote(slot, slot, s_a1.at[c, j], r_a1.at[c, j], pair).wait_recv()
            for k in FAR:
                go(remote(slot, gather[c][k].at[at_j], s_a2.at[c, k, j], r_a2.at[c, k, j], shifted(me, at, a2, k)))
    for c in range(3):
        for t, q in REACH:
            remote(wish, asked_v.at[c, t, q], s_wish.at[c, t, q], r_wish.at[c, t, q], pair).wait_recv()
    loc = pltpu.make_async_copy(asked_v, asked_s, s_loc)
    loc.start()
    loc.wait()
    for k in (0, 1, 3, 2):
        for c, (a1, a2, b) in enumerate(ORDERS):
            row = (at[a2] + 4 - k) % 4
            if k:
                for j in range(4):
                    slot = gather[c][k].at[(at[a1] + 4 - j) % 4]
                    remote(slot, slot, s_a2.at[c, k, j], r_a2.at[c, k, j], pair).wait_recv()
            base = me + (row - at[a2]) * STRIDE[a2] - at[a1] * STRIDE[a1]
            for t, q in REACH + [(0, 0)]:
                for i in range(4):
                    block = gather[c][k][i, asked_s[c, (4 - t) % 4, q, 0, base + i * STRIDE[a1]]]
                    if (t, q) == (0, 0):
                        arrived[c, at[b], core, row, i] = block
                    else:
                        picked[c, t, q, row, i] = block
                if (t, q) != (0, 0):
                    go(remote(picked.at[c, t, q, row], arrived.at[c, at[b], core, row],
                              s_b.at[c, k, t, q], r_b.at[c, k, t, q], column(me, at, core, b, t, q)))
    asked[...] = asked_v[...]
    for k in range(4):
        for c, (a1, a2, b) in enumerate(ORDERS):
            row = (at[a2] + 4 - k) % 4
            for t, q in REACH:
                slot = arrived.at[c, (at[b] + 4 - t) % 4, core + (1 - 2 * core) * q, row]
                remote(slot, slot, s_b.at[c, k, t, q], r_b.at[c, k, t, q], pair).wait_recv()
    for copy in started:
        copy.wait_send()


def fetch(ids, model):
    vmem = pl.BlockSpec(memory_space=pltpu.VMEM)
    smem = pl.BlockSpec(memory_space=pltpu.SMEM)
    f32, i32 = jnp.float32, jnp.int32
    dma = pltpu.SemaphoreType.DMA
    return pl.pallas_call(
        fetch_kernel,
        out_shape=(jax.ShapeDtypeStruct((3, 4, 2, 4, 4, MY, MZ), f32), jax.ShapeDtypeStruct((3, 4, 2, 8, MZ), i32)),
        in_specs=[smem, vmem],
        out_specs=(vmem, vmem),
        scratch_shapes=[
            pltpu.VMEM((8, MZ), i32),
            [[pltpu.VMEM((4, 4, MY, MZ), f32) for k in range(4)] for c in range(3)],
            pltpu.VMEM((3, 4, 2, 4, 4, MY, MZ), f32),
            pltpu.SMEM((3, 4, 2, 8, MZ), i32),
            pltpu.VMEM((3, 4, 2, 8, MZ), i32),
            dma((3, 4, 2)), dma((3, 4, 2)),
            dma((3, 4)), dma((3, 4)),
            dma((3, 4, 4)), dma((3, 4, 4)),
            dma((3, 4, 4, 2)), dma((3, 4, 4, 2)),
            dma,
        ],
        compiler_params=pltpu.CompilerParams(collective_id=0, has_side_effects=True, vmem_limit_bytes=32 * 2**20),
    )(ids, model)


def give_kernel(asked, slots, gradient, landed, part, part_in, row_sum, row_in,
                s_b, r_b, s_a2, r_a2, s_a1, r_a1):
    me, at, core = place()
    pair = other_core(me, core, 1)
    greet(me, at, core)
    started = []

    def go(copy):
        copy.start()
        started.append(copy)

    def landing(c, t, q, row, k, b, device):
        return remote(slots.at[c, (at[b] + t) % 4, core + (1 - 2 * core) * q, row], landed.at[c, t, q, row],
                      s_b.at[c, k, t, q], r_b.at[c, k, t, q], device)

    def rowwise(c, k, j, i, a2):
        return remote(part.at[c, k, i], part_in.at[c, k, i], s_a2.at[c, k, j], r_a2.at[c, k, j], shifted(me, at, a2, k))

    for k in (2, 1, 3, 0):
        for c, (a1, a2, b) in enumerate(ORDERS):
            for t, q in REACH:
                go(landing(c, t, q, (at[a2] + k) % 4, k, b, column(me, at, core, b, t, q)))
    for k in (2, 1, 3, 0):
        for c, (a1, a2, b) in enumerate(ORDERS):
            row = (at[a2] + k) % 4
            for t, q in REACH:
                landing(c, t, q, row, k, b, pair).wait_recv()
            base = me + (row - at[a2]) * STRIDE[a2] - at[a1] * STRIDE[a1]
            for j in (2, 1, 3, 0):
                i = (at[a1] + j) % 4
                own = slots[c, at[b], core, row, i]
                who = asked[c, 0, 0, 0, base + i * STRIDE[a1]]
                total = [jnp.where(who == n, own, 0.0) for n in range(4)]
                for t, q in REACH:
                    term = landed[c, t, q, row, i]
                    who = asked[c, t, q, 0, base + i * STRIDE[a1]]
                    total = [v + jnp.where(who == n, term, 0.0) for n, v in enumerate(total)]
                for n in range(4):
                    part[c, k, i, n] = total[n]
                if k:
                    go(rowwise(c, k, j, i, a2))
    for j in (2, 1, 3, 0):
        for c, (a1, a2, b) in enumerate(ORDERS):
            i = (at[a1] + j) % 4
            for k in FAR:
                rowwise(c, k, j, i, a2).wait_recv()
            for n in range(4):
                row_sum[c, j, n] = (part[c, 0, i, n] + part_in[c, 1, i, n]) + (part_in[c, 2, i, n] + part_in[c, 3, i, n])
            if j:
                go(remote(row_sum.at[c, j], row_in.at[c, j], s_a1.at[c, j], r_a1.at[c, j], shifted(me, at, a1, j)))
    for c, (a1, a2, b) in enumerate(ORDERS):
        for j in FAR:
            remote(row_sum.at[c, j], row_in.at[c, j], s_a1.at[c, j], r_a1.at[c, j], pair).wait_recv()
        for n in range(4):
            gradient[pl.ds(c * 64 + n, MY, stride=4), :] = (row_sum[c, 0, n] + row_in[c, 1, n]) + (row_in[c, 2, n] + row_in[c, 3, n])
    for copy in started:
        copy.wait_send()


def give(asked, slots):
    vmem = pl.BlockSpec(memory_space=pltpu.VMEM)
    smem = pl.BlockSpec(memory_space=pltpu.SMEM)
    f32 = jnp.float32
    dma = pltpu.SemaphoreType.DMA
    return pl.pallas_call(
        give_kernel,
        out_shape=jax.ShapeDtypeStruct((192, MZ), f32),
        in_specs=[smem, vmem],
        out_specs=vmem,
        scratch_shapes=[
            pltpu.VMEM((3, 4, 2, 4, 4, MY, MZ), f32),
            pltpu.VMEM((3, 4, 4, 4, MY, MZ), f32),
            pltpu.VMEM((3, 4, 4, 4, MY, MZ), f32),
            pltpu.VMEM((3, 4, 4, MY, MZ), f32),
            pltpu.VMEM((3, 4, 4, MY, MZ), f32),
            dma((3, 4, 4, 2)), dma((3, 4, 4, 2)),
            dma((3, 4, 4)), dma((3, 4, 4)),
            dma((3, 4)), dma((3, 4)),
        ],
        compiler_params=pltpu.CompilerParams(collective_id=1, has_side_effects=True, vmem_limit_bytes=32 * 2**20),
    )(asked, slots)


def spot(c, block):
    o = block >> 2
    to = {"y": o >> 5, "x": (o >> 3) & 3, "z": (o >> 1) & 3}
    a1, a2, b = ORDERS[c]
    return ((to[b] * 2 + (o & 1)) * 4 + to[a2]) * 4 + to[a1]


def sweep(src, dst, mag, decay, masks, x, visit):
    first, last = masks
    olds = [[s(c, x, 0) for c in range(3)] for s in src]
    befores = [None] * len(src)
    for y in range(MY):
        keep = [decay[c, x, y] for c in range(3)]
        for k in range(len(src)):
            ex, ey, ez = olds[k]
            exz = jnp.where(last, 0.0, pltpu.roll(ex, MZ - 1, 1))
            eyz = jnp.where(last, 0.0, pltpu.roll(ey, MZ - 1, 1))
            eyx, ezx = src[k](1, x + 1, y), src[k](2, x + 1, y)
            h = mag[k]
            if y + 1 < MY:
                nexts = [src[k](c, x, y + 1) for c in range(3)]
                gx = h[0, x + 1, y] + ((nexts[2] - eyz) + (ey - ez))
                gz = h[2, x + 1, y] + ((eyx - nexts[0]) + (ex - ey))
            else:
                nexts = None
                gx = h[0, x + 1, y] + ((ey - ez) - eyz)
                gz = h[2, x + 1, y] + (eyx + (ex - ey))
            gy = h[1, x + 1, y] + ((exz - ezx) + (ez - ex))
            h[0, x + 1, y] = gx
            h[1, x + 1, y] = gy
            h[2, x + 1, y] = gz
            gxz = jnp.where(first, 0.0, pltpu.roll(gx, 1, 1))
            gyz = jnp.where(first, 0.0, pltpu.roll(gy, 1, 1))
            gyx, gzx = h[1, x, y], h[2, x, y]
            if y > 0:
                bx, bz = befores[k]
                cx = (gz - gy) + (gyz - bz)
                cz = (gy - gx) + (bx - gyx)
            else:
                cx = (gz - gy) + gyz
                cz = (gy - gx) - gyx
            cy = (gx - gz) + (gzx - gxz)
            new = [keep[c] * olds[k][c] - 0.25 * v for c, v in enumerate((cx, cy, cz))]
            visit(k, y, olds[k], new)
            befores[k] = (gx, gz)
            olds[k] = nexts


def compute_kernel(entry, weight, near, source, cotangent, fields, slots, hist, mag, decay, grad):
    lane = lax.broadcasted_iota(jnp.int32, (8, MZ), 1)
    masks = (lane == 0, lane == MZ - 1)
    zero = jnp.zeros((MY, 8, MZ), jnp.float32)
    for k in range(2):
        for c in range(3):
            mag[k, c, 0] = zero
            for n in range(HALF + 1):
                hist[k, n, c, MX] = zero

            def clear(x, carry):
                mag[k, c, x + 1] = zero
                return carry
            lax.fori_loop(0, MX, clear, 0)

    def stage(i, carry):
        c, x = i // MX, i % MX
        for y in range(MY):
            row = pl.ds(i * MY + y, 8, stride=3 * MX * MY)
            hist[0, 0, c, x, y] = source[row, :]
            hist[1, 0, c, x, y] = cotangent[row, :]
        return carry
    lax.fori_loop(0, 3 * MX, stage, 0)

    flat_decay = decay.reshape(3 * MX * MY * 8, MZ)
    flat_grad = grad.reshape(3 * MX * MY * 8, MZ)

    def blend(i, carry):
        m, x = i // MX, i % MX
        f = weight[m, x].astype(jnp.float32) * 0.125
        for c in range(3):
            close = near[c, spot(c, entry[m, x])]
            far = near[c, spot(c, entry[m, MX + x])]
            flat_decay[pl.ds((c * MX + x) * (MY * 8) + m, MY, stride=8), :] = 1.0 - 0.5 * (f * close + (1.0 - f) * far)
        return carry
    lax.fori_loop(0, 8 * MX, blend, 0)

    def early(n, carry):
        def plane(x, carry):
            src = [lambda c, xx, y, k=k: hist[k, n, c, xx, y] for k in range(2)]

            def visit(k, y, old, new):
                for c in range(3):
                    hist[k, n + 1, c, x, y] = new[c]
            sweep(src, None, [mag.at[0], mag.at[1]], decay, masks, x, visit)
            return carry
        return lax.fori_loop(0, MX, plane, carry)
    lax.fori_loop(0, HALF, early, 0)

    def late(n, carry):
        def plane(x, carry):
            src = [lambda c, xx, y, k=k: hist[k, HALF, c, xx, y] for k in range(2)]
            part = {}

            def visit(k, y, old, new):
                terms = [old[c] * hist[1 - k, STEPS - 1 - n, c, x, y] for c in range(3)]
                if k == 0:
                    part[y] = terms
                else:
                    for c in range(3):
                        grad[c, x, y] = (grad[c, x, y] if n is not HALF else 0.0) + (part[y][c] + terms[c])
                for c in range(3):
                    hist[k, HALF, c, x, y] = new[c]
            sweep(src, None, [mag.at[0], mag.at[1]], decay, masks, x, visit)
            return carry
        return lax.fori_loop(0, MX, plane, carry)
    late(HALF, 0)
    lax.fori_loop(HALF + 1, STEPS - 1, late, 0)

    def final(x, carry):
        src = [lambda c, xx, y: hist[0, HALF, c, xx, y]]

        def visit(k, y, old, new):
            for c in range(3):
                fields[pl.ds((c * MX + x) * MY + y, 8, stride=3 * MX * MY), :] = new[c]
                grad[c, x, y] = grad[c, x, y] + (old[c] * hist[1, 0, c, x, y] + hist[1, HALF, c, x, y] * hist[0, 0, c, x, y])
        sweep(src, None, [mag.at[0]], decay, masks, x, visit)
        return carry
    lax.fori_loop(0, MX, final, 0)

    def spread(i, carry):
        m, x = i // MX, i % MX
        f = weight[m, x].astype(jnp.float32) * 0.125
        for c in range(3):
            g = flat_grad[pl.ds((c * MX + x) * (MY * 8) + m, MY, stride=8), :]
            slots[c, spot(c, entry[m, x])] = (-0.5 * f) * g
            slots[c, spot(c, entry[m, MX + x])] = (-0.5 * (1.0 - f)) * g
        return carry
    lax.fori_loop(0, 8 * MX, spread, 0)


def compute(entry, weight, near, source, cotangent):
    vmem = pl.BlockSpec(memory_space=pltpu.VMEM)
    smem = pl.BlockSpec(memory_space=pltpu.SMEM)
    f32 = jnp.float32
    return pl.pallas_call(
        compute_kernel,
        out_shape=(jax.ShapeDtypeStruct((8 * 3 * MX * MY, MZ), f32), jax.ShapeDtypeStruct((3, 128, MY, MZ), f32)),
        in_specs=[smem, smem, vmem, vmem, vmem],
        out_specs=(vmem, vmem),
        scratch_shapes=[
            pltpu.VMEM((2, HALF + 1, 3, MX + 1, MY, 8, MZ), f32),
            pltpu.VMEM((2, 3, MX + 1, MY, 8, MZ), f32),
            pltpu.VMEM((3, MX, MY, 8, MZ), f32),
            pltpu.VMEM((3, MX, MY, 8, MZ), f32),
        ],
        compiler_params=pltpu.CompilerParams(vmem_limit_bytes=60 * 2**20),
    )(entry, weight, near, source, cotangent)


def local(conductivity, block_ids, weights, source, cotangent):
    blocks = conductivity.shape[0]
    model = conductivity.reshape(blocks, 3, MY, MZ).transpose(1, 2, 0, 3).reshape(3 * MY * blocks, MZ)
    arrived, asked = fetch(block_ids, model)
    fields, slots = compute(
        block_ids, weights, arrived.reshape(3, 128, MY, MZ), source.reshape(-1, MZ), cotangent.reshape(-1, MZ)
    )
    gradient = give(asked, slots.reshape(arrived.shape))
    gradient = gradient.reshape(3, MY, blocks, MZ).transpose(2, 0, 1, 3)
    return fields.reshape(source.shape), gradient.reshape(conductivity.shape)


def solution(mesh):
    rows = P("dev")
    return jax.shard_map(
        local, mesh=mesh, in_specs=(rows,) * 5, out_specs=(rows, rows), check_vma=False
    )
```

```python
import jax, jax.numpy as jnp
from jax import lax
from jax.experimental import pallas as pl
from jax.experimental.pallas import tpu as pltpu
from jax.sharding import PartitionSpec as P

MX, MY, MZ, STEPS = 8, 16, 128, 10
HALF = STEPS // 2
MESH = pl.DeviceIdType.MESH
STRIDE = {"y": 32, "x": 8, "z": 2}
ORDERS = (("y", "x", "z"), ("x", "z", "y"), ("z", "y", "x"))
FAR = (2, 1, 3)


def place():
    me = lax.axis_index("dev")
    return me, {"y": me // 32, "x": (me // 8) % 4, "z": (me // 2) % 4}, me % 2


def shifted(me, at, dim, k):
    return me + ((at[dim] + k) % 4 - at[dim]) * STRIDE[dim]


def other_core(me, core, q):
    return me + (1 - 2 * core) * q


def column(me, at, core, dim, t, q):
    return other_core(shifted(me, at, dim, t), core, q)


def neighbours(me, at, core):
    out = [other_core(me, core, 1)]
    for dim in ("y", "x", "z"):
        for t in FAR:
            for q in (0, 1):
                out.append(column(me, at, core, dim, t, q))
    return out


def remote(src, dst, send, recv, device):
    return pltpu.make_async_remote_copy(
        src_ref=src, dst_ref=dst, send_sem=send, recv_sem=recv, device_id=(device,), device_id_type=MESH
    )


REACH = [(t, q) for t in (2, 1, 3, 0) for q in (1, 0) if (t, q) != (0, 0)]


def spot(c, block):
    o = block >> 2
    to = {"y": o >> 5, "x": (o >> 3) & 3, "z": (o >> 1) & 3}
    a1, a2, b = ORDERS[c]
    return ((to[b] * 2 + (o & 1)) * 4 + to[a2]) * 4 + to[a1]


def sweep(src, mag, decay, masks, x, visit):
    first, last = masks
    n = len(src)
    olds = [[s(c, x, 0) for c in range(3)] for s in src]
    befores = [None] * n
    queue = []
    for y in range(MY):
        keep = [decay[c, x, y] for c in range(3)]
        stores = []
        nexts = [[src[k](c, x, y + 1) for c in range(3)] if y + 1 < MY else None for k in range(n)]
        ahead = [(src[k](1, x + 1, y), src[k](2, x + 1, y)) for k in range(n)]
        hs = [[mag[k][c, x + 1, y] for c in range(3)] for k in range(n)]
        hb = [(mag[k][1, x, y], mag[k][2, x, y]) for k in range(n)]
        for k in range(n):
            ex, ey, ez = olds[k]
            exz = jnp.where(last, 0.0, pltpu.roll(ex, MZ - 1, 1))
            eyz = jnp.where(last, 0.0, pltpu.roll(ey, MZ - 1, 1))
            eyx, ezx = ahead[k]
            h = mag[k]
            if y + 1 < MY:
                nx = nexts[k]
                gx = hs[k][0] + ((nx[2] - eyz) + (ey - ez))
                gz = hs[k][2] + ((eyx - nx[0]) + (ex - ey))
            else:
                gx = hs[k][0] + ((ey - ez) - eyz)
                gz = hs[k][2] + (eyx + (ex - ey))
            gy = hs[k][1] + ((exz - ezx) + (ez - ex))
            gxz = jnp.where(first, 0.0, pltpu.roll(gx, 1, 1))
            gyz = jnp.where(first, 0.0, pltpu.roll(gy, 1, 1))
            gyx, gzx = hb[k]
            if y > 0:
                bx, bz = befores[k]
                cx = (gz - gy) + (gyz - bz)
                cz = (gy - gx) + (bx - gyx)
            else:
                cx = (gz - gy) + gyz
                cz = (gy - gx) - gyx
            cy = (gx - gz) + (gzx - gxz)
            new = [keep[c] * olds[k][c] - 0.25 * v for c, v in enumerate((cx, cy, cz))]
            def put(k=k, y=y, old=olds[k], new=new, g=(gx, gy, gz)):
                for c in range(3):
                    mag[k][c, x + 1, y] = g[c]
                visit(k, y, old, new)
            stores.append(put)
            befores[k] = (gx, gz)
            olds[k] = nexts[k]
        queue.append(stores)
        if len(queue) > 1:
            for put in queue.pop(0):
                put()
    for stores in queue:
        for put in stores:
            put()


def kernel(ids, weight, model, source, cotangent, fields, gradient,
           wish, gather, picked, arrived, asked_v, asked_s, raw, hist, mag, decay, grad, layer, final_e,
           slots, landed, part, part_in, row_sum, row_in,
           s_raw, s_asked, s_out, s_wish, r_wish, s_a1, r_a1, s_a2, r_a2, s_b, r_b,
           s_gb, r_gb, s_g2, r_g2, s_g1, r_g1):
    me, at, core = place()
    pair = other_core(me, core, 1)
    started = []

    def go(copy):
        copy.start()
        started.append(copy)

    loads = [pltpu.make_async_copy(array, raw.at[k], s_raw.at[k]) for k, array in enumerate((source, cotangent))]
    for load in loads:
        load.start()
    barrier = pltpu.get_barrier_semaphore()
    near = neighbours(me, at, core)
    for other in near:
        pl.semaphore_signal(barrier, inc=1, device_id=(other,), device_id_type=MESH)
    for c, (a1, a2, b) in enumerate(ORDERS):
        for k in range(4):
            gather[c][0][at[a1], k] = model[pl.ds(c * 64 + k, MY, stride=4), :]
    pl.semaphore_wait(barrier, len(near))

    for k in FAR:
        for c, (a1, a2, b) in enumerate(ORDERS):
            own = gather[c][0].at[at[a1]]
            go(remote(own, own, s_a1.at[c, k], r_a1.at[c, k], shifted(me, at, a1, k)))

    def widen(j):
        for c, (a1, a2, b) in enumerate(ORDERS):
            at_j = (at[a1] + 4 - j) % 4
            slot = gather[c][0].at[at_j]
            if j:
                remote(slot, slot, s_a1.at[c, j], r_a1.at[c, j], pair).wait_recv()
            for k in FAR:
                go(remote(slot, gather[c][k].at[at_j], s_a2.at[c, k, j], r_a2.at[c, k, j], shifted(me, at, a2, k)))
    widen(0)

    lane = lax.broadcasted_iota(jnp.int32, (8, MZ), 1)

    def request(m, wanted):
        for i in range(16):
            block = ids[m, i]
            wanted = jnp.where(lane == (block >> 2), (m * 16 + i) * 4 + (block & 3), wanted)
        return wanted
    wanted = lax.fori_loop(0, 8, request, jnp.zeros((8, MZ), jnp.int32))
    wish[...] = wanted
    for c, (a1, a2, b) in enumerate(ORDERS):
        asked_v[c, 0, 0] = wanted
        for t, q in REACH:
            go(remote(wish, asked_v.at[c, t, q], s_wish.at[c, t, q], r_wish.at[c, t, q], column(me, at, core, b, t, q)))
    for j in (1, 3, 2):
        widen(j)
    for c in range(3):
        for t, q in REACH:
            remote(wish, asked_v.at[c, t, q], s_wish.at[c, t, q], r_wish.at[c, t, q], pair).wait_recv()
    loc = pltpu.make_async_copy(asked_v, asked_s, s_asked)
    loc.start()
    loc.wait()

    def place_of(b, side, row):
        return ((b * 2 + side) * 4 + row) * 4

    for k in (0, 1, 3, 2):
        for c, (a1, a2, b) in enumerate(ORDERS):
            row = (at[a2] + 4 - k) % 4
            if k:
                for j in range(4):
                    slot = gather[c][k].at[(at[a1] + 4 - j) % 4]
                    remote(slot, slot, s_a2.at[c, k, j], r_a2.at[c, k, j], pair).wait_recv()
            base = me + (row - at[a2]) * STRIDE[a2] - at[a1] * STRIDE[a1]
            spots = place_of(at[b], core, row)
            for t, q in REACH + [(0, 0)]:
                for i in range(4):
                    block = gather[c][k][i, asked_s[c, (4 - t) % 4, q, 0, base + i * STRIDE[a1]] & 3]
                    if (t, q) == (0, 0):
                        arrived[c, spots + i] = block
                    else:
                        picked[c, t, q, row, i] = block
                if (t, q) != (0, 0):
                    go(remote(picked.at[c, t, q, row], arrived.at[c, pl.ds(spots, 4)],
                              s_b.at[c, k, t, q], r_b.at[c, k, t, q], column(me, at, core, b, t, q)))

    zero = jnp.zeros((8, MZ), jnp.float32)

    def clear(i, carry):
        for c in range(3):
            for k in range(2):
                mag[k, c, i // MY, i % MY] = zero
        return carry
    lax.fori_loop(0, (MX + 1) * MY, clear, 0)

    def clear_grad(i, carry):
        for c in range(3):
            grad[c, i // MY, i % MY] = zero
        return carry
    lax.fori_loop(0, MX * MY, clear_grad, 0)

    def edge(i, carry):
        for y in range(MY):
            for k in range(2):
                for c in (1, 2):
                    hist[k, i, c, MX, y] = zero
        return carry
    lax.fori_loop(0, HALF + 1, edge, 0)
    for load in loads:
        load.wait()

    def stage(i, carry):
        for y in range(MY):
            for k in range(2):
                hist[k, 0, i // MX, i % MX, y] = raw[k, pl.ds(i * MY + y, 8, stride=3 * MX * MY), :]
        return carry
    lax.fori_loop(0, 3 * MX, stage, 0)

    for k in range(4):
        for c, (a1, a2, b) in enumerate(ORDERS):
            row = (at[a2] + 4 - k) % 4
            for t, q in REACH:
                slot = arrived.at[c, pl.ds(place_of((at[b] + 4 - t) % 4, core + (1 - 2 * core) * q, row), 4)]
                remote(slot, slot, s_b.at[c, k, t, q], r_b.at[c, k, t, q], pair).wait_recv()

    flat_decay = decay.reshape(3 * MX * MY * 8, MZ)
    flat_grad = grad.reshape(3 * MX * MY * 8, MZ)

    def blend(i, carry):
        m, x = i // MX, i % MX
        f = weight[m, x].astype(jnp.float32) * 0.125
        for c in range(3):
            close = arrived[c, spot(c, ids[m, x])]
            far = arrived[c, spot(c, ids[m, MX + x])]
            flat_decay[pl.ds((c * MX + x) * (MY * 8) + m, MY, stride=8), :] = 1.0 - 0.5 * (f * close + (1.0 - f) * far)
        return carry
    lax.fori_loop(0, 8 * MX, blend, 0)

    masks = (lane == 0, lane == MZ - 1)

    def early(n, carry):
        def plane(x, carry):
            src = [lambda c, xx, y, k=k: hist[k, n, c, xx, y] for k in range(2)]

            def visit(k, y, old, new):
                for c in range(3):
                    hist[k, n + 1, c, x, y] = new[c]
            sweep(src, [mag.at[0], mag.at[1]], decay, masks, x, visit)
            return carry
        return lax.fori_loop(0, MX, plane, carry)
    lax.fori_loop(0, HALF, early, 0)

    def late(n, carry):
        def plane(x, carry):
            src = [lambda c, xx, y, k=k: hist[k, HALF, c, xx, y] for k in range(2)]
            terms = {}

            def visit(k, y, old, new):
                terms[k] = [old[c] * hist[1 - k, STEPS - 1 - n, c, x, y] for c in range(3)]
                for c in range(3):
                    if k == 1:
                        grad[c, x, y] = grad[c, x, y] + (terms[0][c] + terms[1][c])
                    hist[k, HALF, c, x, y] = new[c]
            sweep(src, [mag.at[0], mag.at[1]], decay, masks, x, visit)
            return carry
        return lax.fori_loop(0, MX, plane, carry)
    lax.fori_loop(HALF, STEPS - 1, late, 0)

    def final(x, carry):
        src = [lambda c, xx, y: hist[0, HALF, c, xx, y]]

        def visit(k, y, old, new):
            for c in range(3):
                final_e[pl.ds((c * MX + x) * MY + y, 8, stride=3 * MX * MY), :] = new[c]
                grad[c, x, y] = grad[c, x, y] + (old[c] * hist[1, 0, c, x, y] + hist[1, HALF, c, x, y] * hist[0, 0, c, x, y])
        sweep(src, [mag.at[0]], decay, masks, x, visit)
        return carry
    lax.fori_loop(0, MX, final, 0)
    save = pltpu.make_async_copy(final_e, fields, s_out)
    save.start()

    def unstage(i, carry):
        for m in range(8):
            layer[i * 8 + m] = flat_grad[pl.ds(i * (MY * 8) + m, MY, stride=8), :]
        return carry
    lax.fori_loop(0, 3 * MX, unstage, 0)

    def landing(c, t, q, row, k, b, device):
        spots = place_of((at[b] + t) % 4, core + (1 - 2 * core) * q, row)
        return remote(slots.at[c, pl.ds(spots, 4)], landed.at[c, t, q, row], s_gb.at[c, k, t, q], r_gb.at[c, k, t, q], device)

    def rowwise(c, k, j, i, a2):
        return remote(part.at[c, k, i], part_in.at[c, k, i], s_g2.at[c, k, j], r_g2.at[c, k, j], shifted(me, at, a2, k))

    for k in (2, 1, 3, 0):
        for c, (a1, a2, b) in enumerate(ORDERS):
            row = (at[a2] + k) % 4
            for t, q in REACH + [(0, 0)]:
                side = core + (1 - 2 * core) * q
                to = (at[b] + t) % 4
                base = to * STRIDE[b] + side + row * STRIDE[a2]
                for i in range(4):
                    e = asked_s[c, 0, 0, 0, base + i * STRIDE[a1]] >> 2
                    x = e & 7
                    f = weight[e >> 4, x].astype(jnp.float32) * 0.125
                    scale = jnp.where((e & 8) == 0, f, 1.0 - f) * -0.5
                    slots[c, place_of(to, side, row) + i] = scale * layer[(c * MX + x) * 8 + (e >> 4)]
                if (t, q) != (0, 0):
                    go(landing(c, t, q, row, k, b, column(me, at, core, b, t, q)))
    for k in (2, 1, 3, 0):
        for c, (a1, a2, b) in enumerate(ORDERS):
            row = (at[a2] + k) % 4
            for t, q in REACH:
                landing(c, t, q, row, k, b, pair).wait_recv()
            base = me + (row - at[a2]) * STRIDE[a2] - at[a1] * STRIDE[a1]
            for j in (2, 1, 3, 0):
                i = (at[a1] + j) % 4
                who = asked_s[c, 0, 0, 0, base + i * STRIDE[a1]] & 3
                own = slots[c, place_of(at[b], core, row) + i]
                total = [jnp.where(who == n, own, 0.0) for n in range(4)]
                for t, q in REACH:
                    who = asked_s[c, t, q, 0, base + i * STRIDE[a1]] & 3
                    term = landed[c, t, q, row, i]
                    total = [v + jnp.where(who == n, term, 0.0) for n, v in enumerate(total)]
                for n in range(4):
                    part[c, k, i, n] = total[n]
                if k:
                    go(rowwise(c, k, j, i, a2))
    for j in (2, 1, 3, 0):
        for c, (a1, a2, b) in enumerate(ORDERS):
            i = (at[a1] + j) % 4
            for k in FAR:
                rowwise(c, k, j, i, a2).wait_recv()
            for n in range(4):
                row_sum[c, j, n] = (part[c, 0, i, n] + part_in[c, 1, i, n]) + (part_in[c, 2, i, n] + part_in[c, 3, i, n])
            if j:
                go(remote(row_sum.at[c, j], row_in.at[c, j], s_g1.at[c, j], r_g1.at[c, j], shifted(me, at, a1, j)))
    for c in range(3):
        for j in FAR:
            remote(row_sum.at[c, j], row_in.at[c, j], s_g1.at[c, j], r_g1.at[c, j], pair).wait_recv()
        for n in range(4):
            gradient[pl.ds(c * 64 + n, MY, stride=4), :] = (row_sum[c, 0, n] + row_in[c, 1, n]) + (row_in[c, 2, n] + row_in[c, 3, n])
    for copy in started:
        copy.wait_send()
    save.wait()


def run(ids, weight, model, source, cotangent):
    vmem = pl.BlockSpec(memory_space=pltpu.VMEM)
    smem = pl.BlockSpec(memory_space=pltpu.SMEM)
    anywhere = pl.BlockSpec(memory_space=pl.ANY)
    f32, i32 = jnp.float32, jnp.int32
    dma = pltpu.SemaphoreType.DMA
    rows = 8 * 3 * MX * MY
    return pl.pallas_call(
        kernel,
        out_shape=(jax.ShapeDtypeStruct((rows, MZ), f32), jax.ShapeDtypeStruct((192, MZ), f32)),
        in_specs=[smem, smem, vmem, anywhere, anywhere],
        out_specs=(anywhere, vmem),
        scratch_shapes=[
            pltpu.VMEM((8, MZ), i32),
            [[pltpu.VMEM((4, 4, MY, MZ), f32) for k in range(4)] for c in range(3)],
            pltpu.VMEM((3, 4, 2, 4, 4, MY, MZ), f32),
            pltpu.VMEM((3, 128, MY, MZ), f32),
            pltpu.VMEM((3, 4, 2, 8, MZ), i32),
            pltpu.SMEM((3, 4, 2, 8, MZ), i32),
            pltpu.VMEM((2, rows, MZ), f32),
            pltpu.VMEM((2, HALF + 1, 3, MX + 1, MY, 8, MZ), f32),
            pltpu.VMEM((2, 3, MX + 1, MY, 8, MZ), f32),
            pltpu.VMEM((3, MX, MY, 8, MZ), f32),
            pltpu.VMEM((3, MX, MY, 8, MZ), f32),
            pltpu.VMEM((3 * MX * 8, MY, MZ), f32),
            pltpu.VMEM((rows, MZ), f32),
            pltpu.VMEM((3, 128, MY, MZ), f32),
            pltpu.VMEM((3, 4, 2, 4, 4, MY, MZ), f32),
            pltpu.VMEM((3, 4, 4, 4, MY, MZ), f32),
            pltpu.VMEM((3, 4, 4, 4, MY, MZ), f32),
            pltpu.VMEM((3, 4, 4, MY, MZ), f32),
            pltpu.VMEM((3, 4, 4, MY, MZ), f32),
            dma((2,)), dma, dma,
            dma((3, 4, 2)), dma((3, 4, 2)),
            dma((3, 4)), dma((3, 4)),
            dma((3, 4, 4)), dma((3, 4, 4)),
            dma((3, 4, 4, 2)), dma((3, 4, 4, 2)),
            dma((3, 4, 4, 2)), dma((3, 4, 4, 2)),
            dma((3, 4, 4)), dma((3, 4, 4)),
            dma((3, 4)), dma((3, 4)),
        ],
        compiler_params=pltpu.CompilerParams(collective_id=0, has_side_effects=True, vmem_limit_bytes=57 * 2**20),
    )(ids, weight, model, source, cotangent)


def local(conductivity, block_ids, weights, source, cotangent):
    blocks = conductivity.shape[0]
    model = conductivity.reshape(blocks, 3, MY, MZ).transpose(1, 2, 0, 3).reshape(3 * MY * blocks, MZ)
    fields, gradient = run(block_ids, weights, model, source.reshape(-1, MZ), cotangent.reshape(-1, MZ))
    gradient = gradient.reshape(3, MY, blocks, MZ).transpose(2, 0, 1, 3)
    return fields.reshape(source.shape), gradient.reshape(conductivity.shape)


def solution(mesh):
    rows = P("dev")
    return jax.shard_map(
        local, mesh=mesh, in_specs=(rows,) * 5, out_specs=(rows, rows), check_vma=False
    )
```

```python
import jax, jax.numpy as jnp
from jax import lax
from jax.experimental import pallas as pl
from jax.experimental.pallas import tpu as pltpu
from jax.sharding import PartitionSpec as P

MX, MY, MZ, STEPS = 8, 16, 128, 10
HALF = STEPS // 2
MESH = pl.DeviceIdType.MESH
STRIDE = {"y": 32, "x": 8, "z": 2}
ORDERS = (("y", "x", "z"), ("x", "z", "y"), ("z", "y", "x"))
FAR = (2, 1, 3)


def place():
    me = lax.axis_index("dev")
    return me, {"y": me // 32, "x": (me // 8) % 4, "z": (me // 2) % 4}, me % 2


def shifted(me, at, dim, k):
    return me + ((at[dim] + k) % 4 - at[dim]) * STRIDE[dim]


def other_core(me, core, q):
    return me + (1 - 2 * core) * q


def column(me, at, core, dim, t, q):
    return other_core(shifted(me, at, dim, t), core, q)


def neighbours(me, at, core):
    out = [other_core(me, core, 1)]
    for dim in ("y", "x", "z"):
        for t in FAR:
            for q in (0, 1):
                out.append(column(me, at, core, dim, t, q))
    return out


def remote(src, dst, send, recv, device):
    return pltpu.make_async_remote_copy(
        src_ref=src, dst_ref=dst, send_sem=send, recv_sem=recv, device_id=(device,), device_id_type=MESH
    )


REACH = [(t, q) for t in (2, 1, 3, 0) for q in (1, 0) if (t, q) != (0, 0)]


def spot(c, block):
    o = block >> 2
    to = {"y": o >> 5, "x": (o >> 3) & 3, "z": (o >> 1) & 3}
    a1, a2, b = ORDERS[c]
    return ((to[b] * 2 + (o & 1)) * 4 + to[a2]) * 4 + to[a1]


def sweep(src, mag, decay, masks, x, visit, first_stage=True, second_stage=True):
    first, last = masks
    n = len(src)
    p = x + 1
    if first_stage:
        olds = [[s(c, p, 0) for c in range(3)] for s in src]
    befores = [None] * n
    for y in range(MY):
        if first_stage:
            stores = []
            for k in range(n):
                ex, ey, ez = olds[k]
                nx = [src[k](c, p, y + 1) for c in range(3)] if y + 1 < MY else None
                eyx, ezx = src[k](1, p + 1, y), src[k](2, p + 1, y)
                exz = jnp.where(last, 0.0, pltpu.roll(ex, MZ - 1, 1))
                eyz = jnp.where(last, 0.0, pltpu.roll(ey, MZ - 1, 1))
                h = mag[k]
                if y + 1 < MY:
                    gx = h[0, p + 1, y] + ((nx[2] - eyz) + (ey - ez))
                    gz = h[2, p + 1, y] + ((eyx - nx[0]) + (ex - ey))
                else:
                    gx = h[0, p + 1, y] + ((ey - ez) - eyz)
                    gz = h[2, p + 1, y] + (eyx + (ex - ey))
                gy = h[1, p + 1, y] + ((exz - ezx) + (ez - ex))
                olds[k] = nx
                stores.append((h, gx, gy, gz))
        if second_stage:
            keep = [decay[c, x, y] for c in range(3)]
            outs = []
            for k in range(n):
                h = mag[k]
                gx, gy, gz = (h[c, x + 1, y] for c in range(3))
                old = [src[k](c, x, y) for c in range(3)]
                gxz = jnp.where(first, 0.0, pltpu.roll(gx, 1, 1))
                gyz = jnp.where(first, 0.0, pltpu.roll(gy, 1, 1))
                gyx, gzx = h[1, x, y], h[2, x, y]
                if y > 0:
                    bx, bz = befores[k]
                    cx = (gz - gy) + (gyz - bz)
                    cz = (gy - gx) + (bx - gyx)
                else:
                    cx = (gz - gy) + gyz
                    cz = (gy - gx) - gyx
                cy = (gx - gz) + (gzx - gxz)
                new = [keep[c] * old[c] - 0.25 * v for c, v in enumerate((cx, cy, cz))]
                befores[k] = (gx, gz)
                outs.append((k, y, old, new))
        if first_stage:
            for h, gx, gy, gz in stores:
                h[0, p + 1, y] = gx
                h[1, p + 1, y] = gy
                h[2, p + 1, y] = gz
        if second_stage:
            for o in outs:
                visit(*o)


def kernel(ids, weight, model, source, cotangent, fields, gradient,
           wish, gather, picked, arrived, asked_v, asked_s, raw, hist, cur, mag, decay, grad, layer,
           slots, landed, part, part_in, row_sum, row_in,
           s_raw, s_asked, s_wish, r_wish, s_a1, r_a1, s_a2, r_a2, s_b, r_b,
           s_gb, r_gb, s_g2, r_g2, s_g1, r_g1):
    me, at, core = place()
    pair = other_core(me, core, 1)
    started = []

    def go(copy):
        copy.start()
        started.append(copy)

    loads = [pltpu.make_async_copy(array, raw.at[k], s_raw.at[k]) for k, array in enumerate((source, cotangent))]
    for load in loads:
        load.start()
    barrier = pltpu.get_barrier_semaphore()
    near = neighbours(me, at, core)
    for other in near:
        pl.semaphore_signal(barrier, inc=1, device_id=(other,), device_id_type=MESH)
    for c, (a1, a2, b) in enumerate(ORDERS):
        for k in range(4):
            gather[c][0][at[a1], k] = model[pl.ds(c * 64 + k, MY, stride=4), :]
    pl.semaphore_wait(barrier, len(near))

    for k in FAR:
        for c, (a1, a2, b) in enumerate(ORDERS):
            own = gather[c][0].at[at[a1]]
            go(remote(own, own, s_a1.at[c, k], r_a1.at[c, k], shifted(me, at, a1, k)))

    def widen(j):
        for c, (a1, a2, b) in enumerate(ORDERS):
            at_j = (at[a1] + 4 - j) % 4
            slot = gather[c][0].at[at_j]
            if j:
                remote(slot, slot, s_a1.at[c, j], r_a1.at[c, j], pair).wait_recv()
            for k in FAR:
                go(remote(slot, gather[c][k].at[at_j], s_a2.at[c, k, j], r_a2.at[c, k, j], shifted(me, at, a2, k)))
    widen(0)

    lane = lax.broadcasted_iota(jnp.int32, (8, MZ), 1)

    def request(m, wanted):
        for i in range(16):
            block = ids[m, i]
            wanted = jnp.where(lane == (block >> 2), (m * 16 + i) * 4 + (block & 3), wanted)
        return wanted
    wanted = lax.fori_loop(0, 8, request, jnp.zeros((8, MZ), jnp.int32))
    wish[...] = wanted
    for c, (a1, a2, b) in enumerate(ORDERS):
        asked_v[c, 0, 0] = wanted
        for t, q in REACH:
            go(remote(wish, asked_v.at[c, t, q], s_wish.at[c, t, q], r_wish.at[c, t, q], column(me, at, core, b, t, q)))
    for j in (1, 3, 2):
        widen(j)
    for c in range(3):
        for t, q in REACH:
            remote(wish, asked_v.at[c, t, q], s_wish.at[c, t, q], r_wish.at[c, t, q], pair).wait_recv()
    loc = pltpu.make_async_copy(asked_v, asked_s, s_asked)
    loc.start()
    loc.wait()

    def place_of(b, side, row):
        return ((b * 2 + side) * 4 + row) * 4

    for k in (0, 1, 3, 2):
        for c, (a1, a2, b) in enumerate(ORDERS):
            row = (at[a2] + 4 - k) % 4
            if k:
                for j in range(4):
                    slot = gather[c][k].at[(at[a1] + 4 - j) % 4]
                    remote(slot, slot, s_a2.at[c, k, j], r_a2.at[c, k, j], pair).wait_recv()
            base = me + (row - at[a2]) * STRIDE[a2] - at[a1] * STRIDE[a1]
            spots = place_of(at[b], core, row)
            for t, q in REACH + [(0, 0)]:
                for i in range(4):
                    block = gather[c][k][i, asked_s[c, (4 - t) % 4, q, 0, base + i * STRIDE[a1]] & 3]
                    if (t, q) == (0, 0):
                        arrived[c, spots + i] = block
                    else:
                        picked[c, t, q, row, i] = block
                if (t, q) != (0, 0):
                    go(remote(picked.at[c, t, q, row], arrived.at[c, pl.ds(spots, 4)],
                              s_b.at[c, k, t, q], r_b.at[c, k, t, q], column(me, at, core, b, t, q)))

    zero = jnp.zeros((8, MZ), jnp.float32)

    def clear(i, carry):
        for c in range(3):
            for k in range(2):
                mag[k, c, i // MY, i % MY] = zero
        return carry
    lax.fori_loop(0, (MX + 1) * MY, clear, 0)

    def clear_grad(i, carry):
        for c in range(3):
            grad[c, i // MY, i % MY] = zero
        return carry
    lax.fori_loop(0, MX * MY, clear_grad, 0)

    for y in range(MY):
        for k in range(2):
            for c in (1, 2):
                cur[k, c, MX, y] = zero
    for load in loads:
        load.wait()

    def stage(i, carry):
        for y in range(MY):
            for k in range(2):
                cur[k, i // MX, i % MX, y] = raw[k, pl.ds(i * MY + y, 8, stride=3 * MX * MY), :]
        return carry
    lax.fori_loop(0, 3 * MX, stage, 0)

    for k in range(4):
        for c, (a1, a2, b) in enumerate(ORDERS):
            row = (at[a2] + 4 - k) % 4
            for t, q in REACH:
                slot = arrived.at[c, pl.ds(place_of((at[b] + 4 - t) % 4, core + (1 - 2 * core) * q, row), 4)]
                remote(slot, slot, s_b.at[c, k, t, q], r_b.at[c, k, t, q], pair).wait_recv()

    flat_decay = decay.reshape(3 * MX * MY * 8, MZ)
    flat_grad = grad.reshape(3 * MX * MY * 8, MZ)

    def blend(i, carry):
        m, x = i // MX, i % MX
        f = weight[m, x].astype(jnp.float32) * 0.125
        for c in range(3):
            close = arrived[c, spot(c, ids[m, x])]
            far = arrived[c, spot(c, ids[m, MX + x])]
            flat_decay[pl.ds((c * MX + x) * (MY * 8) + m, MY, stride=8), :] = 1.0 - 0.5 * (f * close + (1.0 - f) * far)
        return carry
    lax.fori_loop(0, 8 * MX, blend, 0)

    masks = (lane == 0, lane == MZ - 1)

    state = [lambda c, x, y, k=k: cur[k, c, x, y] for k in range(2)]
    mags = [mag.at[k] for k in range(2)]

    def early(n, carry):
        def plane(x, carry, **which):
            def visit(k, y, old, new):
                for c in range(3):
                    hist[k, n, c, x, y] = old[c]
                    cur[k, c, x, y] = new[c]
            sweep(state, mags, decay, masks, x, visit, **which)
            return carry
        plane(-1, 0, second_stage=False)
        lax.fori_loop(0, MX - 1, plane, carry)
        plane(MX - 1, 0, first_stage=False)
        return carry
    lax.fori_loop(0, HALF, early, 0)

    def late(n, carry):
        def plane(x, carry, **which):
            terms = {}

            def visit(k, y, old, new):
                terms[k] = [old[c] * hist[1 - k, STEPS - 1 - n, c, x, y] for c in range(3)]
                for c in range(3):
                    if k == 1:
                        grad[c, x, y] = grad[c, x, y] + (terms[0][c] + terms[1][c])
                    cur[k, c, x, y] = new[c]
            sweep(state, mags, decay, masks, x, visit, **which)
            return carry
        plane(-1, 0, second_stage=False)
        lax.fori_loop(0, MX - 1, plane, carry)
        plane(MX - 1, 0, first_stage=False)
        return carry
    lax.fori_loop(HALF, STEPS - 1, late, 0)

    def final(carry):
        def plane(x, carry, **which):
            def visit(k, y, old, new):
                for c in range(3):
                    fields[pl.ds((c * MX + x) * MY + y, 8, stride=3 * MX * MY), :] = new[c]
                    grad[c, x, y] = grad[c, x, y] + (old[c] * hist[1, 0, c, x, y] + cur[1, c, x, y] * hist[0, 0, c, x, y])
            sweep(state[:1], mags[:1], decay, masks, x, visit, **which)
            return carry
        plane(-1, 0, second_stage=False)
        lax.fori_loop(0, MX - 1, plane, carry)
        plane(MX - 1, 0, first_stage=False)
        return carry
    final(0)

    def unstage(i, carry):
        for m in range(8):
            layer[i * 8 + m] = flat_grad[pl.ds(i * (MY * 8) + m, MY, stride=8), :]
        return carry
    lax.fori_loop(0, 3 * MX, unstage, 0)

    def landing(c, t, q, row, k, b, device):
        spots = place_of((at[b] + t) % 4, core + (1 - 2 * core) * q, row)
        return remote(slots.at[c, pl.ds(spots, 4)], landed.at[c, t, q, row], s_gb.at[c, k, t, q], r_gb.at[c, k, t, q], device)

    def rowwise(c, k, j, i, a2):
        return remote(part.at[c, k, i], part_in.at[c, k, i], s_g2.at[c, k, j], r_g2.at[c, k, j], shifted(me, at, a2, k))

    for k in (2, 1, 3, 0):
        for c, (a1, a2, b) in enumerate(ORDERS):
            row = (at[a2] + k) % 4
            for t, q in REACH + [(0, 0)]:
                side = core + (1 - 2 * core) * q
                to = (at[b] + t) % 4
                base = to * STRIDE[b] + side + row * STRIDE[a2]
                for i in range(4):
                    e = asked_s[c, 0, 0, 0, base + i * STRIDE[a1]] >> 2
                    x = e & 7
                    f = weight[e >> 4, x].astype(jnp.float32) * 0.125
                    scale = jnp.where((e & 8) == 0, f, 1.0 - f) * -0.5
                    slots[c, place_of(to, side, row) + i] = scale * layer[(c * MX + x) * 8 + (e >> 4)]
                if (t, q) != (0, 0):
                    go(landing(c, t, q, row, k, b, column(me, at, core, b, t, q)))
    for k in (2, 1, 3, 0):
        for c, (a1, a2, b) in enumerate(ORDERS):
            row = (at[a2] + k) % 4
            for t, q in REACH:
                landing(c, t, q, row, k, b, pair).wait_recv()
            base = me + (row - at[a2]) * STRIDE[a2] - at[a1] * STRIDE[a1]
            for j in (2, 1, 3, 0):
                i = (at[a1] + j) % 4
                who = asked_s[c, 0, 0, 0, base + i * STRIDE[a1]] & 3
                own = slots[c, place_of(at[b], core, row) + i]
                total = [jnp.where(who == n, own, 0.0) for n in range(4)]
                for t, q in REACH:
                    who = asked_s[c, t, q, 0, base + i * STRIDE[a1]] & 3
                    term = landed[c, t, q, row, i]
                    total = [v + jnp.where(who == n, term, 0.0) for n, v in enumerate(total)]
                for n in range(4):
                    part[c, k, i, n] = total[n]
                if k:
                    go(rowwise(c, k, j, i, a2))
    for j in (2, 1, 3, 0):
        for c, (a1, a2, b) in enumerate(ORDERS):
            i = (at[a1] + j) % 4
            for k in FAR:
                rowwise(c, k, j, i, a2).wait_recv()
            for n in range(4):
                row_sum[c, j, n] = (part[c, 0, i, n] + part_in[c, 1, i, n]) + (part_in[c, 2, i, n] + part_in[c, 3, i, n])
            if j:
                go(remote(row_sum.at[c, j], row_in.at[c, j], s_g1.at[c, j], r_g1.at[c, j], shifted(me, at, a1, j)))
    for c in range(3):
        for j in FAR:
            remote(row_sum.at[c, j], row_in.at[c, j], s_g1.at[c, j], r_g1.at[c, j], pair).wait_recv()
        for n in range(4):
            gradient[pl.ds(c * 64 + n, MY, stride=4), :] = (row_sum[c, 0, n] + row_in[c, 1, n]) + (row_in[c, 2, n] + row_in[c, 3, n])
    for copy in started:
        copy.wait_send()


def run(ids, weight, model, source, cotangent):
    vmem = pl.BlockSpec(memory_space=pltpu.VMEM)
    smem = pl.BlockSpec(memory_space=pltpu.SMEM)
    anywhere = pl.BlockSpec(memory_space=pl.ANY)
    f32, i32 = jnp.float32, jnp.int32
    dma = pltpu.SemaphoreType.DMA
    rows = 8 * 3 * MX * MY
    return pl.pallas_call(
        kernel,
        out_shape=(jax.ShapeDtypeStruct((rows, MZ), f32), jax.ShapeDtypeStruct((192, MZ), f32)),
        in_specs=[smem, smem, vmem, anywhere, anywhere],
        out_specs=(vmem, vmem),
        scratch_shapes=[
            pltpu.VMEM((8, MZ), i32),
            [[pltpu.VMEM((4, 4, MY, MZ), f32) for k in range(4)] for c in range(3)],
            pltpu.VMEM((3, 4, 2, 4, 4, MY, MZ), f32),
            pltpu.VMEM((3, 128, MY, MZ), f32),
            pltpu.VMEM((3, 4, 2, 8, MZ), i32),
            pltpu.SMEM((3, 4, 2, 8, MZ), i32),
            pltpu.VMEM((2, rows, MZ), f32),
            pltpu.VMEM((2, HALF, 3, MX, MY, 8, MZ), f32),
            pltpu.VMEM((2, 3, MX + 1, MY, 8, MZ), f32),
            pltpu.VMEM((2, 3, MX + 1, MY, 8, MZ), f32),
            pltpu.VMEM((3, MX, MY, 8, MZ), f32),
            pltpu.VMEM((3, MX, MY, 8, MZ), f32),
            pltpu.VMEM((3 * MX * 8, MY, MZ), f32),
            pltpu.VMEM((3, 128, MY, MZ), f32),
            pltpu.VMEM((3, 4, 2, 4, 4, MY, MZ), f32),
            pltpu.VMEM((3, 4, 4, 4, MY, MZ), f32),
            pltpu.VMEM((3, 4, 4, 4, MY, MZ), f32),
            pltpu.VMEM((3, 4, 4, MY, MZ), f32),
            pltpu.VMEM((3, 4, 4, MY, MZ), f32),
            dma((2,)), dma,
            dma((3, 4, 2)), dma((3, 4, 2)),
            dma((3, 4)), dma((3, 4)),
            dma((3, 4, 4)), dma((3, 4, 4)),
            dma((3, 4, 4, 2)), dma((3, 4, 4, 2)),
            dma((3, 4, 4, 2)), dma((3, 4, 4, 2)),
            dma((3, 4, 4)), dma((3, 4, 4)),
            dma((3, 4)), dma((3, 4)),
        ],
        compiler_params=pltpu.CompilerParams(collective_id=0, has_side_effects=True, vmem_limit_bytes=51 * 2**20),
    )(ids, weight, model, source, cotangent)


def local(conductivity, block_ids, weights, source, cotangent):
    blocks = conductivity.shape[0]
    model = conductivity.reshape(blocks, 3, MY, MZ).transpose(1, 2, 0, 3).reshape(3 * MY * blocks, MZ)
    fields, gradient = run(block_ids, weights, model, source.reshape(-1, MZ), cotangent.reshape(-1, MZ))
    gradient = gradient.reshape(3, MY, blocks, MZ).transpose(2, 0, 1, 3)
    return fields.reshape(source.shape), gradient.reshape(conductivity.shape)


def solution(mesh):
    rows = P("dev")
    return jax.shard_map(
        local, mesh=mesh, in_specs=(rows,) * 5, out_specs=(rows, rows), check_vma=False
    )
```

```python
import jax, jax.numpy as jnp
from jax import lax
from jax.experimental import pallas as pl
from jax.experimental.pallas import tpu as pltpu
from jax.sharding import PartitionSpec as P

MX, MY, MZ, STEPS = 8, 16, 128, 10
HALF = STEPS // 2
MESH = pl.DeviceIdType.MESH
STRIDE = {"y": 32, "x": 8, "z": 2}
ORDERS = (("y", "x", "z"), ("x", "z", "y"), ("z", "y", "x"))
FAR = (2, 1, 3)


def place():
    me = lax.axis_index("dev")
    return me, {"y": me // 32, "x": (me // 8) % 4, "z": (me // 2) % 4}, me % 2


def shifted(me, at, dim, k):
    return me + ((at[dim] + k) % 4 - at[dim]) * STRIDE[dim]


def other_core(me, core, q):
    return me + (1 - 2 * core) * q


def column(me, at, core, dim, t, q):
    return other_core(shifted(me, at, dim, t), core, q)


def neighbours(me, at, core):
    out = [other_core(me, core, 1)]
    for dim in ("y", "x", "z"):
        for t in FAR:
            for q in (0, 1):
                out.append(column(me, at, core, dim, t, q))
    return out


def remote(src, dst, send, recv, device):
    return pltpu.make_async_remote_copy(
        src_ref=src, dst_ref=dst, send_sem=send, recv_sem=recv, device_id=(device,), device_id_type=MESH
    )


REACH = [(t, q) for t in (2, 1, 3, 0) for q in (1, 0) if (t, q) != (0, 0)]


def spot(c, block):
    o = block >> 2
    to = {"y": o >> 5, "x": (o >> 3) & 3, "z": (o >> 1) & 3}
    a1, a2, b = ORDERS[c]
    return ((to[b] * 2 + (o & 1)) * 4 + to[a2]) * 4 + to[a1]


def sweep(src, mag, decay, masks, x, visit, first_stage=True, second_stage=True):
    first, last = masks
    n = len(src)
    p = x + 1
    if first_stage:
        olds = [[s(c, p, 0) for c in range(3)] for s in src]
    befores = [None] * n
    for y in range(MY):
        if first_stage:
            stores = []
            for k in range(n):
                ex, ey, ez = olds[k]
                nx = [src[k](c, p, y + 1) for c in range(3)] if y + 1 < MY else None
                eyx, ezx = src[k](1, p + 1, y), src[k](2, p + 1, y)
                exz = jnp.where(last, 0.0, pltpu.roll(ex, MZ - 1, 1))
                eyz = jnp.where(last, 0.0, pltpu.roll(ey, MZ - 1, 1))
                h = mag[k]
                if y + 1 < MY:
                    gx = h[0, p + 1, y] + ((nx[2] - eyz) + (ey - ez))
                    gz = h[2, p + 1, y] + ((eyx - nx[0]) + (ex - ey))
                else:
                    gx = h[0, p + 1, y] + ((ey - ez) - eyz)
                    gz = h[2, p + 1, y] + (eyx + (ex - ey))
                gy = h[1, p + 1, y] + ((exz - ezx) + (ez - ex))
                olds[k] = nx
                stores.append((h, gx, gy, gz))
        if second_stage:
            keep = [decay[c, x, y] for c in range(3)]
            outs = []
            for k in range(n):
                h = mag[k]
                gx, gy, gz = (h[c, x + 1, y] for c in range(3))
                old = [src[k](c, x, y) for c in range(3)]
                gxz = jnp.where(first, 0.0, pltpu.roll(gx, 1, 1))
                gyz = jnp.where(first, 0.0, pltpu.roll(gy, 1, 1))
                gyx, gzx = h[1, x, y], h[2, x, y]
                if y > 0:
                    bx, bz = befores[k]
                    cx = (gz - gy) + (gyz - bz)
                    cz = (gy - gx) + (bx - gyx)
                else:
                    cx = (gz - gy) + gyz
                    cz = (gy - gx) - gyx
                cy = (gx - gz) + (gzx - gxz)
                new = [keep[c] * old[c] - 0.25 * v for c, v in enumerate((cx, cy, cz))]
                befores[k] = (gx, gz)
                outs.append((k, y, old, new))
        if first_stage:
            for h, gx, gy, gz in stores:
                h[0, p + 1, y] = gx
                h[1, p + 1, y] = gy
                h[2, p + 1, y] = gz
        if second_stage:
            for o in outs:
                visit(*o)


def kernel(ids, weight, model, source, cotangent, fields, gradient,
           wish, gather, picked, arrived, asked_v, asked_s, raw, hist, cur, mag, decay, grad, layer,
           slots, landed, part, part_in, row_sum, row_in,
           s_raw, s_asked, s_wish, r_wish, s_a1, r_a1, s_a2, r_a2, s_b, r_b,
           s_gb, r_gb, s_g2, r_g2, s_g1, r_g1):
    me, at, core = place()
    pair = other_core(me, core, 1)
    started = []

    def go(copy):
        copy.start()
        started.append(copy)

    loads = [pltpu.make_async_copy(array, raw.at[k], s_raw.at[k]) for k, array in enumerate((source, cotangent))]
    for load in loads:
        load.start()
    barrier = pltpu.get_barrier_semaphore()
    near = neighbours(me, at, core)
    for other in near:
        pl.semaphore_signal(barrier, inc=1, device_id=(other,), device_id_type=MESH)
    for c, (a1, a2, b) in enumerate(ORDERS):
        for k in range(4):
            gather[c][0][at[a1], k] = model[pl.ds(c * 64 + k, MY, stride=4), :]
    pl.semaphore_wait(barrier, len(near))

    for k in FAR:
        for c, (a1, a2, b) in enumerate(ORDERS):
            own = gather[c][0].at[at[a1]]
            go(remote(own, own, s_a1.at[c, k], r_a1.at[c, k], shifted(me, at, a1, k)))

    def widen(j):
        for c, (a1, a2, b) in enumerate(ORDERS):
            at_j = (at[a1] + 4 - j) % 4
            slot = gather[c][0].at[at_j]
            if j:
                remote(slot, slot, s_a1.at[c, j], r_a1.at[c, j], pair).wait_recv()
            for k in FAR:
                go(remote(slot, gather[c][k].at[at_j], s_a2.at[c, k, j], r_a2.at[c, k, j], shifted(me, at, a2, k)))
    widen(0)

    lane = lax.broadcasted_iota(jnp.int32, (8, MZ), 1)

    def request(m, wanted):
        for i in range(16):
            block = ids[m, i]
            wanted = jnp.where(lane == (block >> 2), (m * 16 + i) * 4 + (block & 3), wanted)
        return wanted
    wanted = lax.fori_loop(0, 8, request, jnp.zeros((8, MZ), jnp.int32))
    wish[...] = wanted
    for c, (a1, a2, b) in enumerate(ORDERS):
        asked_v[c, 0, 0] = wanted
        for t, q in REACH:
            go(remote(wish, asked_v.at[c, t, q], s_wish.at[c, t, q], r_wish.at[c, t, q], column(me, at, core, b, t, q)))
    for j in (1, 3, 2):
        widen(j)
    for c in range(3):
        for t, q in REACH:
            remote(wish, asked_v.at[c, t, q], s_wish.at[c, t, q], r_wish.at[c, t, q], pair).wait_recv()
    loc = pltpu.make_async_copy(asked_v, asked_s, s_asked)
    loc.start()
    loc.wait()

    def place_of(b, side, row):
        return ((b * 2 + side) * 4 + row) * 4

    for k in (0, 1, 3, 2):
        for c, (a1, a2, b) in enumerate(ORDERS):
            row = (at[a2] + 4 - k) % 4
            if k:
                for j in range(4):
                    slot = gather[c][k].at[(at[a1] + 4 - j) % 4]
                    remote(slot, slot, s_a2.at[c, k, j], r_a2.at[c, k, j], pair).wait_recv()
            base = me + (row - at[a2]) * STRIDE[a2] - at[a1] * STRIDE[a1]
            spots = place_of(at[b], core, row)
            for t, q in REACH + [(0, 0)]:
                for i in range(4):
                    block = gather[c][k][i, asked_s[c, (4 - t) % 4, q, 0, base + i * STRIDE[a1]] & 3]
                    if (t, q) == (0, 0):
                        arrived[c, spots + i] = block
                    else:
                        picked[c, t, q, row, i] = block
                if (t, q) != (0, 0):
                    go(remote(picked.at[c, t, q, row], arrived.at[c, pl.ds(spots, 4)],
                              s_b.at[c, k, t, q], r_b.at[c, k, t, q], column(me, at, core, b, t, q)))

    zero = jnp.zeros((8, MZ), jnp.float32)

    def clear(i, carry):
        for c in range(3):
            for k in range(2):
                mag[k, c, i // MY, i % MY] = zero
        return carry
    lax.fori_loop(0, (MX + 1) * MY, clear, 0)

    def clear_grad(i, carry):
        for c in range(3):
            grad[c, i // MY, i % MY] = zero
            decay[c, i // MY, i % MY] = zero
        return carry
    lax.fori_loop(0, MX * MY, clear_grad, 0)

    for y in range(MY):
        for k in range(2):
            for c in (1, 2):
                cur[k, c, MX, y] = zero
    for load in loads:
        load.wait()

    def stage(i, carry):
        for y in range(MY):
            for k in range(2):
                cur[k, i // MX, i % MX, y] = raw[k, pl.ds(i * MY + y, 8, stride=3 * MX * MY), :]
        return carry
    lax.fori_loop(0, 3 * MX, stage, 0)

    masks = (lane == 0, lane == MZ - 1)
    state = [lambda c, x, y, k=k: cur[k, c, x, y] for k in range(2)]
    mags = [mag.at[k] for k in range(2)]

    def early(n, carry):
        def plane(x, carry, **which):
            def visit(k, y, old, new):
                for c in range(3):
                    hist[k, n, c, x, y] = old[c]
                    cur[k, c, x, y] = new[c]
            sweep(state, mags, decay, masks, x, visit, **which)
            return carry
        plane(-1, 0, second_stage=False)
        lax.fori_loop(0, MX - 1, plane, carry)
        plane(MX - 1, 0, first_stage=False)
        return carry

    lax.fori_loop(0, 1, early, 0)

    for k in range(4):
        for c, (a1, a2, b) in enumerate(ORDERS):
            row = (at[a2] + 4 - k) % 4
            for t, q in REACH:
                slot = arrived.at[c, pl.ds(place_of((at[b] + 4 - t) % 4, core + (1 - 2 * core) * q, row), 4)]
                remote(slot, slot, s_b.at[c, k, t, q], r_b.at[c, k, t, q], pair).wait_recv()

    flat_decay = decay.reshape(3 * MX * MY * 8, MZ)
    flat_grad = grad.reshape(3 * MX * MY * 8, MZ)

    def blend(i, carry):
        m, x = i // MX, i % MX
        f = weight[m, x].astype(jnp.float32) * 0.125
        for c in range(3):
            close = arrived[c, spot(c, ids[m, x])]
            far = arrived[c, spot(c, ids[m, MX + x])]
            flat_decay[pl.ds((c * MX + x) * (MY * 8) + m, MY, stride=8), :] = 1.0 - 0.5 * (f * close + (1.0 - f) * far)
        return carry
    lax.fori_loop(0, 8 * MX, blend, 0)

    def damp(i, carry):
        c, x = i // MX, i % MX
        for y in range(MY):
            for k in range(2):
                cur[k, c, x, y] = decay[c, x, y] * hist[k, 0, c, x, y] + cur[k, c, x, y]
        return carry
    lax.fori_loop(0, 3 * MX, damp, 0)
    lax.fori_loop(1, HALF, early, 0)

    def late(n, carry):
        def plane(x, carry, **which):
            terms = {}

            def visit(k, y, old, new):
                terms[k] = [old[c] * hist[1 - k, STEPS - 1 - n, c, x, y] for c in range(3)]
                for c in range(3):
                    if k == 1:
                        grad[c, x, y] = grad[c, x, y] + (terms[0][c] + terms[1][c])
                    cur[k, c, x, y] = new[c]
            sweep(state, mags, decay, masks, x, visit, **which)
            return carry
        plane(-1, 0, second_stage=False)
        lax.fori_loop(0, MX - 1, plane, carry)
        plane(MX - 1, 0, first_stage=False)
        return carry
    lax.fori_loop(HALF, STEPS - 1, late, 0)

    def unstage(i, carry):
        c, x = i // MX, i % MX
        for y in range(MY):
            grad[c, x, y] = grad[c, x, y] + (cur[0, c, x, y] * hist[1, 0, c, x, y] + cur[1, c, x, y] * hist[0, 0, c, x, y])
        for m in range(8):
            layer[i * 8 + m] = flat_grad[pl.ds(i * (MY * 8) + m, MY, stride=8), :]
        return carry
    lax.fori_loop(0, 3 * MX, unstage, 0)

    def landing(c, t, q, row, k, b, device):
        spots = place_of((at[b] + t) % 4, core + (1 - 2 * core) * q, row)
        return remote(slots.at[c, pl.ds(spots, 4)], landed.at[c, t, q, row], s_gb.at[c, k, t, q], r_gb.at[c, k, t, q], device)

    def rowwise(c, k, j, i, a2):
        return remote(part.at[c, k, i], part_in.at[c, k, i], s_g2.at[c, k, j], r_g2.at[c, k, j], shifted(me, at, a2, k))

    for k in (2, 1, 3, 0):
        for c, (a1, a2, b) in enumerate(ORDERS):
            row = (at[a2] + k) % 4
            for t, q in REACH + [(0, 0)]:
                side = core + (1 - 2 * core) * q
                to = (at[b] + t) % 4
                base = to * STRIDE[b] + side + row * STRIDE[a2]
                for i in range(4):
                    e = asked_s[c, 0, 0, 0, base + i * STRIDE[a1]] >> 2
                    x = e & 7
                    f = weight[e >> 4, x].astype(jnp.float32) * 0.125
                    scale = jnp.where((e & 8) == 0, f, 1.0 - f) * -0.5
                    slots[c, place_of(to, side, row) + i] = scale * layer[(c * MX + x) * 8 + (e >> 4)]
                if (t, q) != (0, 0):
                    go(landing(c, t, q, row, k, b, column(me, at, core, b, t, q)))

    def final(carry):
        def plane(x, carry, **which):
            def visit(k, y, old, new):
                for c in range(3):
                    fields[pl.ds((c * MX + x) * MY + y, 8, stride=3 * MX * MY), :] = new[c]
            sweep(state[:1], mags[:1], decay, masks, x, visit, **which)
            return carry
        plane(-1, 0, second_stage=False)
        lax.fori_loop(0, MX - 1, plane, carry)
        plane(MX - 1, 0, first_stage=False)
        return carry
    final(0)

    for k in (2, 1, 3, 0):
        for c, (a1, a2, b) in enumerate(ORDERS):
            row = (at[a2] + k) % 4
            for t, q in REACH:
                landing(c, t, q, row, k, b, pair).wait_recv()
            base = me + (row - at[a2]) * STRIDE[a2] - at[a1] * STRIDE[a1]
            for j in (2, 1, 3, 0):
                i = (at[a1] + j) % 4
                who = asked_s[c, 0, 0, 0, base + i * STRIDE[a1]] & 3
                own = slots[c, place_of(at[b], core, row) + i]
                total = [jnp.where(who == n, own, 0.0) for n in range(4)]
                for t, q in REACH:
                    who = asked_s[c, t, q, 0, base + i * STRIDE[a1]] & 3
                    term = landed[c, t, q, row, i]
                    total = [v + jnp.where(who == n, term, 0.0) for n, v in enumerate(total)]
                for n in range(4):
                    part[c, k, i, n] = total[n]
                if k:
                    go(rowwise(c, k, j, i, a2))
    for j in (2, 1, 3, 0):
        for c, (a1, a2, b) in enumerate(ORDERS):
            i = (at[a1] + j) % 4
            for k in FAR:
                rowwise(c, k, j, i, a2).wait_recv()
            for n in range(4):
                row_sum[c, j, n] = (part[c, 0, i, n] + part_in[c, 1, i, n]) + (part_in[c, 2, i, n] + part_in[c, 3, i, n])
            if j:
                go(remote(row_sum.at[c, j], row_in.at[c, j], s_g1.at[c, j], r_g1.at[c, j], shifted(me, at, a1, j)))
    for c in range(3):
        for j in FAR:
            remote(row_sum.at[c, j], row_in.at[c, j], s_g1.at[c, j], r_g1.at[c, j], pair).wait_recv()
        for n in range(4):
            gradient[pl.ds(c * 64 + n, MY, stride=4), :] = (row_sum[c, 0, n] + row_in[c, 1, n]) + (row_in[c, 2, n] + row_in[c, 3, n])
    for copy in started:
        copy.wait_send()


def run(ids, weight, model, source, cotangent):
    vmem = pl.BlockSpec(memory_space=pltpu.VMEM)
    smem = pl.BlockSpec(memory_space=pltpu.SMEM)
    anywhere = pl.BlockSpec(memory_space=pl.ANY)
    f32, i32 = jnp.float32, jnp.int32
    dma = pltpu.SemaphoreType.DMA
    rows = 8 * 3 * MX * MY
    return pl.pallas_call(
        kernel,
        out_shape=(jax.ShapeDtypeStruct((rows, MZ), f32), jax.ShapeDtypeStruct((192, MZ), f32)),
        in_specs=[smem, smem, vmem, anywhere, anywhere],
        out_specs=(vmem, vmem),
        scratch_shapes=[
            pltpu.VMEM((8, MZ), i32),
            [[pltpu.VMEM((4, 4, MY, MZ), f32) for k in range(4)] for c in range(3)],
            pltpu.VMEM((3, 4, 2, 4, 4, MY, MZ), f32),
            pltpu.VMEM((3, 128, MY, MZ), f32),
            pltpu.VMEM((3, 4, 2, 8, MZ), i32),
            pltpu.SMEM((3, 4, 2, 8, MZ), i32),
            pltpu.VMEM((2, rows, MZ), f32),
            pltpu.VMEM((2, HALF, 3, MX, MY, 8, MZ), f32),
            pltpu.VMEM((2, 3, MX + 1, MY, 8, MZ), f32),
            pltpu.VMEM((2, 3, MX + 1, MY, 8, MZ), f32),
            pltpu.VMEM((3, MX, MY, 8, MZ), f32),
            pltpu.VMEM((3, MX, MY, 8, MZ), f32),
            pltpu.VMEM((3 * MX * 8, MY, MZ), f32),
            pltpu.VMEM((3, 128, MY, MZ), f32),
            pltpu.VMEM((3, 4, 2, 4, 4, MY, MZ), f32),
            pltpu.VMEM((3, 4, 4, 4, MY, MZ), f32),
            pltpu.VMEM((3, 4, 4, 4, MY, MZ), f32),
            pltpu.VMEM((3, 4, 4, MY, MZ), f32),
            pltpu.VMEM((3, 4, 4, MY, MZ), f32),
            dma((2,)), dma,
            dma((3, 4, 2)), dma((3, 4, 2)),
            dma((3, 4)), dma((3, 4)),
            dma((3, 4, 4)), dma((3, 4, 4)),
            dma((3, 4, 4, 2)), dma((3, 4, 4, 2)),
            dma((3, 4, 4, 2)), dma((3, 4, 4, 2)),
            dma((3, 4, 4)), dma((3, 4, 4)),
            dma((3, 4)), dma((3, 4)),
        ],
        compiler_params=pltpu.CompilerParams(collective_id=0, has_side_effects=True, vmem_limit_bytes=51 * 2**20),
    )(ids, weight, model, source, cotangent)


def local(conductivity, block_ids, weights, source, cotangent):
    blocks = conductivity.shape[0]
    model = conductivity.reshape(blocks, 3, MY, MZ).transpose(1, 2, 0, 3).reshape(3 * MY * blocks, MZ)
    fields, gradient = run(block_ids, weights, model, source.reshape(-1, MZ), cotangent.reshape(-1, MZ))
    gradient = gradient.reshape(3, MY, blocks, MZ).transpose(2, 0, 1, 3)
    return fields.reshape(source.shape), gradient.reshape(conductivity.shape)


def solution(mesh):
    rows = P("dev")
    return jax.shard_map(
        local, mesh=mesh, in_specs=(rows,) * 5, out_specs=(rows, rows), check_vma=False
    )
```

```python
import jax, jax.numpy as jnp
from jax import lax
from jax.experimental import pallas as pl
from jax.experimental.pallas import tpu as pltpu
from jax.sharding import PartitionSpec as P

MX, MY, MZ, STEPS = 8, 16, 128, 10
HALF = STEPS // 2
MESH = pl.DeviceIdType.MESH
STRIDE = {"y": 32, "x": 8, "z": 2}
ORDERS = (("y", "x", "z"), ("x", "z", "y"), ("z", "y", "x"))
FAR = (2, 1, 3)


def place():
    me = lax.axis_index("dev")
    return me, {"y": me // 32, "x": (me // 8) % 4, "z": (me // 2) % 4}, me % 2


def shifted(me, at, dim, k):
    return me + ((at[dim] + k) % 4 - at[dim]) * STRIDE[dim]


def other_core(me, core, q):
    return me + (1 - 2 * core) * q


def column(me, at, core, dim, t, q):
    return other_core(shifted(me, at, dim, t), core, q)


def neighbours(me, at, core):
    out = [other_core(me, core, 1)]
    for dim in ("y", "x", "z"):
        for t in FAR:
            for q in (0, 1):
                out.append(column(me, at, core, dim, t, q))
    return out


def remote(src, dst, send, recv, device):
    return pltpu.make_async_remote_copy(
        src_ref=src, dst_ref=dst, send_sem=send, recv_sem=recv, device_id=(device,), device_id_type=MESH
    )


REACH = [(t, q) for t in (2, 1, 3, 0) for q in (1, 0) if (t, q) != (0, 0)]


def spot(c, block):
    o = block >> 2
    to = {"y": o >> 5, "x": (o >> 3) & 3, "z": (o >> 1) & 3}
    a1, a2, b = ORDERS[c]
    return ((to[b] * 2 + (o & 1)) * 4 + to[a2]) * 4 + to[a1]


def sweep(src, mag, decay, masks, x, visit, first_stage=True, second_stage=True):
    first, last = masks
    n = len(src)
    p = x + 1
    if first_stage:
        olds = [[s(c, p, 0) for c in range(3)] for s in src]
    befores = [None] * n
    for y in range(MY):
        if first_stage:
            stores = []
            for k in range(n):
                ex, ey, ez = olds[k]
                nx = [src[k](c, p, y + 1) for c in range(3)] if y + 1 < MY else None
                eyx, ezx = src[k](1, p + 1, y), src[k](2, p + 1, y)
                exz = jnp.where(last, 0.0, pltpu.roll(ex, MZ - 1, 1))
                eyz = jnp.where(last, 0.0, pltpu.roll(ey, MZ - 1, 1))
                h = mag[k]
                if y + 1 < MY:
                    gx = h[0, p + 1, y] + ((nx[2] - eyz) + (ey - ez))
                    gz = h[2, p + 1, y] + ((eyx - nx[0]) + (ex - ey))
                else:
                    gx = h[0, p + 1, y] + ((ey - ez) - eyz)
                    gz = h[2, p + 1, y] + (eyx + (ex - ey))
                gy = h[1, p + 1, y] + ((exz - ezx) + (ez - ex))
                olds[k] = nx
                stores.append((h, gx, gy, gz))
        if second_stage:
            keep = [decay[c, x, y] for c in range(3)]
            outs = []
            for k in range(n):
                h = mag[k]
                gx, gy, gz = (h[c, x + 1, y] for c in range(3))
                old = [src[k](c, x, y) for c in range(3)]
                gxz = jnp.where(first, 0.0, pltpu.roll(gx, 1, 1))
                gyz = jnp.where(first, 0.0, pltpu.roll(gy, 1, 1))
                gyx, gzx = h[1, x, y], h[2, x, y]
                if y > 0:
                    bx, bz = befores[k]
                    cx = (gz - gy) + (gyz - bz)
                    cz = (gy - gx) + (bx - gyx)
                else:
                    cx = (gz - gy) + gyz
                    cz = (gy - gx) - gyx
                cy = (gx - gz) + (gzx - gxz)
                new = [keep[c] * old[c] - 0.25 * v for c, v in enumerate((cx, cy, cz))]
                befores[k] = (gx, gz)
                outs.append((k, y, old, new))
        if first_stage:
            for h, gx, gy, gz in stores:
                h[0, p + 1, y] = gx
                h[1, p + 1, y] = gy
                h[2, p + 1, y] = gz
        if second_stage:
            for o in outs:
                visit(*o)


def kernel(ids, model, source, cotangent, fields, gradient,
           wish, gather, picked, arrived, asked_v, asked_s, raw, hist, cur, mag, decay, grad, layer,
           slots, landed, part, part_in, row_sum, row_in,
           s_raw, s_asked, s_wish, r_wish, s_a1, r_a1, s_a2, r_a2, s_b, r_b,
           s_gb, r_gb, s_g2, r_g2, s_g1, r_g1):
    me, at, core = place()
    pair = other_core(me, core, 1)
    started = []

    def go(copy):
        copy.start()
        started.append(copy)

    loads = [pltpu.make_async_copy(array, raw.at[k], s_raw.at[k]) for k, array in enumerate((source, cotangent))]
    for load in loads:
        load.start()
    barrier = pltpu.get_barrier_semaphore()
    near = neighbours(me, at, core)
    for other in near:
        pl.semaphore_signal(barrier, inc=1, device_id=(other,), device_id_type=MESH)
    for c, (a1, a2, b) in enumerate(ORDERS):
        for k in range(4):
            gather[c][0][at[a1], k] = model[pl.ds(c * 64 + k, MY, stride=4), :]
    pl.semaphore_wait(barrier, len(near))

    for k in FAR:
        for c, (a1, a2, b) in enumerate(ORDERS):
            own = gather[c][0].at[at[a1]]
            go(remote(own, own, s_a1.at[c, k], r_a1.at[c, k], shifted(me, at, a1, k)))

    def widen(j):
        for c, (a1, a2, b) in enumerate(ORDERS):
            at_j = (at[a1] + 4 - j) % 4
            slot = gather[c][0].at[at_j]
            if j:
                remote(slot, slot, s_a1.at[c, j], r_a1.at[c, j], pair).wait_recv()
            for k in FAR:
                go(remote(slot, gather[c][k].at[at_j], s_a2.at[c, k, j], r_a2.at[c, k, j], shifted(me, at, a2, k)))
    widen(0)

    lane = lax.broadcasted_iota(jnp.int32, (8, MZ), 1)

    def request(m, wanted):
        for i in range(16):
            block = ids[m, i]
            wanted = jnp.where(lane == (block >> 2), (m * 16 + i) * 4 + (block & 3), wanted)
        return wanted
    wanted = lax.fori_loop(0, 8, request, jnp.zeros((8, MZ), jnp.int32))
    wish[...] = wanted
    for c, (a1, a2, b) in enumerate(ORDERS):
        asked_v[c, 0, 0] = wanted
        for t, q in REACH:
            go(remote(wish, asked_v.at[c, t, q], s_wish.at[c, t, q], r_wish.at[c, t, q], column(me, at, core, b, t, q)))
    for j in (1, 3, 2):
        widen(j)
    for c in range(3):
        for t, q in REACH:
            remote(wish, asked_v.at[c, t, q], s_wish.at[c, t, q], r_wish.at[c, t, q], pair).wait_recv()
    loc = pltpu.make_async_copy(asked_v, asked_s, s_asked)
    loc.start()
    loc.wait()

    def place_of(b, side, row):
        return ((b * 2 + side) * 4 + row) * 4

    for k in (0, 1, 3, 2):
        for c, (a1, a2, b) in enumerate(ORDERS):
            row = (at[a2] + 4 - k) % 4
            if k:
                for j in range(4):
                    slot = gather[c][k].at[(at[a1] + 4 - j) % 4]
                    remote(slot, slot, s_a2.at[c, k, j], r_a2.at[c, k, j], pair).wait_recv()
            base = me + (row - at[a2]) * STRIDE[a2] - at[a1] * STRIDE[a1]
            spots = place_of(at[b], core, row)
            for t, q in REACH + [(0, 0)]:
                for i in range(4):
                    block = gather[c][k][i, asked_s[c, (4 - t) % 4, q, 0, base + i * STRIDE[a1]] & 3]
                    if (t, q) == (0, 0):
                        arrived[c, spots + i] = block
                    else:
                        picked[c, t, q, row, i] = block
                if (t, q) != (0, 0):
                    go(remote(picked.at[c, t, q, row], arrived.at[c, pl.ds(spots, 4)],
                              s_b.at[c, k, t, q], r_b.at[c, k, t, q], column(me, at, core, b, t, q)))

    zero = jnp.zeros((8, MZ), jnp.float32)

    def clear(i, carry):
        for c in range(3):
            for k in range(2):
                mag[k, c, i // MY, i % MY] = zero
        return carry
    lax.fori_loop(0, (MX + 1) * MY, clear, 0)

    def clear_grad(i, carry):
        for c in range(3):
            grad[c, i // MY, i % MY] = zero
            decay[c, i // MY, i % MY] = zero
        return carry
    lax.fori_loop(0, MX * MY, clear_grad, 0)

    for y in range(MY):
        for k in range(2):
            for c in (1, 2):
                cur[k, c, MX, y] = zero
    for load in loads:
        load.wait()

    def stage(i, carry):
        for y in range(MY):
            for k in range(2):
                cur[k, i // MX, i % MX, y] = raw[k, pl.ds(i * MY + y, 8, stride=3 * MX * MY), :]
        return carry
    lax.fori_loop(0, 3 * MX, stage, 0)

    masks = (lane == 0, lane == MZ - 1)
    state = [lambda c, x, y, k=k: cur[k, c, x, y] for k in range(2)]
    mags = [mag.at[k] for k in range(2)]

    def early(n, carry):
        def plane(x, carry, **which):
            def visit(k, y, old, new):
                for c in range(3):
                    hist[k, n, c, x, y] = old[c]
                    cur[k, c, x, y] = new[c]
            sweep(state, mags, decay, masks, x, visit, **which)
            return carry
        plane(-1, 0, second_stage=False)
        lax.fori_loop(0, MX - 1, plane, carry)
        plane(MX - 1, 0, first_stage=False)
        return carry

    lax.fori_loop(0, 1, early, 0)

    for k in range(4):
        for c, (a1, a2, b) in enumerate(ORDERS):
            row = (at[a2] + 4 - k) % 4
            for t, q in REACH:
                slot = arrived.at[c, pl.ds(place_of((at[b] + 4 - t) % 4, core + (1 - 2 * core) * q, row), 4)]
                remote(slot, slot, s_b.at[c, k, t, q], r_b.at[c, k, t, q], pair).wait_recv()

    flat_decay = decay.reshape(3 * MX * MY * 8, MZ)
    flat_grad = grad.reshape(3 * MX * MY * 8, MZ)

    def blend(i, carry):
        m, x = i // MX, i % MX
        f = ids[m, 2 * MX + x].astype(jnp.float32) * 0.125
        for c in range(3):
            close = arrived[c, spot(c, ids[m, x])]
            far = arrived[c, spot(c, ids[m, MX + x])]
            flat_decay[pl.ds((c * MX + x) * (MY * 8) + m, MY, stride=8), :] = 1.0 - 0.5 * (f * close + (1.0 - f) * far)
        return carry
    lax.fori_loop(0, 8 * MX, blend, 0)

    def damp(i, carry):
        c, x = i // MX, i % MX
        for y in range(MY):
            for k in range(2):
                cur[k, c, x, y] = decay[c, x, y] * hist[k, 0, c, x, y] + cur[k, c, x, y]
        return carry
    lax.fori_loop(0, 3 * MX, damp, 0)
    lax.fori_loop(1, HALF, early, 0)

    def late(n, carry):
        def plane(x, carry, **which):
            terms = {}

            def visit(k, y, old, new):
                terms[k] = [old[c] * hist[1 - k, STEPS - 1 - n, c, x, y] for c in range(3)]
                for c in range(3):
                    if k == 1:
                        grad[c, x, y] = grad[c, x, y] + (terms[0][c] + terms[1][c])
                    cur[k, c, x, y] = new[c]
            sweep(state, mags, decay, masks, x, visit, **which)
            return carry
        plane(-1, 0, second_stage=False)
        lax.fori_loop(0, MX - 1, plane, carry)
        plane(MX - 1, 0, first_stage=False)
        return carry
    lax.fori_loop(HALF, STEPS - 1, late, 0)

    def unstage(i, carry):
        c, x = i // MX, i % MX
        for y in range(MY):
            grad[c, x, y] = grad[c, x, y] + (cur[0, c, x, y] * hist[1, 0, c, x, y] + cur[1, c, x, y] * hist[0, 0, c, x, y])
        for m in range(8):
            layer[i * 8 + m] = flat_grad[pl.ds(i * (MY * 8) + m, MY, stride=8), :]
        return carry
    lax.fori_loop(0, 3 * MX, unstage, 0)

    def landing(c, t, q, row, k, b, device):
        spots = place_of((at[b] + t) % 4, core + (1 - 2 * core) * q, row)
        return remote(slots.at[c, pl.ds(spots, 4)], landed.at[c, t, q, row], s_gb.at[c, k, t, q], r_gb.at[c, k, t, q], device)

    def rowwise(c, k, j, i, a2):
        return remote(part.at[c, k, i], part_in.at[c, k, i], s_g2.at[c, k, j], r_g2.at[c, k, j], shifted(me, at, a2, k))

    for k in (2, 1, 3, 0):
        for c, (a1, a2, b) in enumerate(ORDERS):
            row = (at[a2] + k) % 4
            for t, q in REACH + [(0, 0)]:
                side = core + (1 - 2 * core) * q
                to = (at[b] + t) % 4
                base = to * STRIDE[b] + side + row * STRIDE[a2]
                for i in range(4):
                    e = asked_s[c, 0, 0, 0, base + i * STRIDE[a1]] >> 2
                    x = e & 7
                    f = ids[e >> 4, 2 * MX + x].astype(jnp.float32) * 0.125
                    scale = jnp.where((e & 8) == 0, f, 1.0 - f) * -0.5
                    slots[c, place_of(to, side, row) + i] = scale * layer[(c * MX + x) * 8 + (e >> 4)]
                if (t, q) != (0, 0):
                    go(landing(c, t, q, row, k, b, column(me, at, core, b, t, q)))

    def final(carry):
        def plane(x, carry, **which):
            def visit(k, y, old, new):
                for c in range(3):
                    fields[pl.ds((c * MX + x) * MY + y, 8, stride=3 * MX * MY), :] = new[c]
            sweep(state[:1], mags[:1], decay, masks, x, visit, **which)
            return carry
        plane(-1, 0, second_stage=False)
        lax.fori_loop(0, MX - 1, plane, carry)
        plane(MX - 1, 0, first_stage=False)
        return carry
    final(0)

    for k in (2, 1, 3, 0):
        for c, (a1, a2, b) in enumerate(ORDERS):
            row = (at[a2] + k) % 4
            for t, q in REACH:
                landing(c, t, q, row, k, b, pair).wait_recv()
            base = me + (row - at[a2]) * STRIDE[a2] - at[a1] * STRIDE[a1]
            for j in (2, 1, 3, 0):
                i = (at[a1] + j) % 4
                who = asked_s[c, 0, 0, 0, base + i * STRIDE[a1]] & 3
                own = slots[c, place_of(at[b], core, row) + i]
                total = [jnp.where(who == n, own, 0.0) for n in range(4)]
                for t, q in REACH:
                    who = asked_s[c, t, q, 0, base + i * STRIDE[a1]] & 3
                    term = landed[c, t, q, row, i]
                    total = [v + jnp.where(who == n, term, 0.0) for n, v in enumerate(total)]
                for n in range(4):
                    part[c, k, i, n] = total[n]
                if k:
                    go(rowwise(c, k, j, i, a2))
    for j in (2, 1, 3, 0):
        for c, (a1, a2, b) in enumerate(ORDERS):
            i = (at[a1] + j) % 4
            for k in FAR:
                rowwise(c, k, j, i, a2).wait_recv()
            for n in range(4):
                row_sum[c, j, n] = (part[c, 0, i, n] + part_in[c, 1, i, n]) + (part_in[c, 2, i, n] + part_in[c, 3, i, n])
            if j:
                go(remote(row_sum.at[c, j], row_in.at[c, j], s_g1.at[c, j], r_g1.at[c, j], shifted(me, at, a1, j)))
    for c in range(3):
        for j in FAR:
            remote(row_sum.at[c, j], row_in.at[c, j], s_g1.at[c, j], r_g1.at[c, j], pair).wait_recv()
        for n in range(4):
            gradient[pl.ds(c * 64 + n, MY, stride=4), :] = (row_sum[c, 0, n] + row_in[c, 1, n]) + (row_in[c, 2, n] + row_in[c, 3, n])
    for copy in started:
        copy.wait_send()


def run(ids, model, source, cotangent):
    vmem = pl.BlockSpec(memory_space=pltpu.VMEM)
    smem = pl.BlockSpec(memory_space=pltpu.SMEM)
    anywhere = pl.BlockSpec(memory_space=pl.ANY)
    f32, i32 = jnp.float32, jnp.int32
    dma = pltpu.SemaphoreType.DMA
    rows = 8 * 3 * MX * MY
    return pl.pallas_call(
        kernel,
        out_shape=(jax.ShapeDtypeStruct((rows, MZ), f32), jax.ShapeDtypeStruct((192, MZ), f32)),
        in_specs=[smem, vmem, anywhere, anywhere],
        out_specs=(vmem, vmem),
        scratch_shapes=[
            pltpu.VMEM((8, MZ), i32),
            [[pltpu.VMEM((4, 4, MY, MZ), f32) for k in range(4)] for c in range(3)],
            pltpu.VMEM((3, 4, 2, 4, 4, MY, MZ), f32),
            pltpu.VMEM((3, 128, MY, MZ), f32),
            pltpu.VMEM((3, 4, 2, 8, MZ), i32),
            pltpu.SMEM((3, 4, 2, 8, MZ), i32),
            pltpu.VMEM((2, rows, MZ), f32),
            pltpu.VMEM((2, HALF, 3, MX, MY, 8, MZ), f32),
            pltpu.VMEM((2, 3, MX + 1, MY, 8, MZ), f32),
            pltpu.VMEM((2, 3, MX + 1, MY, 8, MZ), f32),
            pltpu.VMEM((3, MX, MY, 8, MZ), f32),
            pltpu.VMEM((3, MX, MY, 8, MZ), f32),
            pltpu.VMEM((3 * MX * 8, MY, MZ), f32),
            pltpu.VMEM((3, 128, MY, MZ), f32),
            pltpu.VMEM((3, 4, 2, 4, 4, MY, MZ), f32),
            pltpu.VMEM((3, 4, 4, 4, MY, MZ), f32),
            pltpu.VMEM((3, 4, 4, 4, MY, MZ), f32),
            pltpu.VMEM((3, 4, 4, MY, MZ), f32),
            pltpu.VMEM((3, 4, 4, MY, MZ), f32),
            dma((2,)), dma,
            dma((3, 4, 2)), dma((3, 4, 2)),
            dma((3, 4)), dma((3, 4)),
            dma((3, 4, 4)), dma((3, 4, 4)),
            dma((3, 4, 4, 2)), dma((3, 4, 4, 2)),
            dma((3, 4, 4, 2)), dma((3, 4, 4, 2)),
            dma((3, 4, 4)), dma((3, 4, 4)),
            dma((3, 4)), dma((3, 4)),
        ],
        compiler_params=pltpu.CompilerParams(collective_id=0, has_side_effects=True, vmem_limit_bytes=51 * 2**20),
    )(ids, model, source, cotangent)


def local(conductivity, block_ids, weights, source, cotangent):
    blocks = conductivity.shape[0]
    model = conductivity.reshape(blocks, 3, MY, MZ).transpose(1, 2, 0, 3).reshape(3 * MY * blocks, MZ)
    fields, gradient = run(jnp.concatenate([block_ids, weights], axis=1), model, source.reshape(-1, MZ), cotangent.reshape(-1, MZ))
    gradient = gradient.reshape(3, MY, blocks, MZ).transpose(2, 0, 1, 3)
    return fields.reshape(source.shape), gradient.reshape(conductivity.shape)


def solution(mesh):
    rows = P("dev")
    return jax.shard_map(
        local, mesh=mesh, in_specs=(rows,) * 5, out_specs=(rows, rows), check_vma=False
    )
```

```python
import jax, jax.numpy as jnp
from jax import lax
from jax.experimental import pallas as pl
from jax.experimental.pallas import tpu as pltpu
from jax.sharding import PartitionSpec as P

MX, MY, MZ, STEPS = 8, 16, 128, 10
HALF = STEPS // 2
MESH = pl.DeviceIdType.MESH
STRIDE = {"y": 32, "x": 8, "z": 2}
ORDERS = (("y", "x", "z"), ("x", "z", "y"), ("z", "y", "x"))
FAR = (2, 1, 3)


def place():
    me = lax.axis_index("dev")
    return me, {"y": me // 32, "x": (me // 8) % 4, "z": (me // 2) % 4}, me % 2


def shifted(me, at, dim, k):
    return me + ((at[dim] + k) % 4 - at[dim]) * STRIDE[dim]


def other_core(me, core, q):
    return me + (1 - 2 * core) * q


def column(me, at, core, dim, t, q):
    return other_core(shifted(me, at, dim, t), core, q)


def neighbours(me, at, core):
    out = [other_core(me, core, 1)]
    for dim in ("y", "x", "z"):
        for t in FAR:
            for q in (0, 1):
                out.append(column(me, at, core, dim, t, q))
    return out


def remote(src, dst, send, recv, device):
    return pltpu.make_async_remote_copy(
        src_ref=src, dst_ref=dst, send_sem=send, recv_sem=recv, device_id=(device,), device_id_type=MESH
    )


REACH = [(t, q) for t in (2, 1, 3, 0) for q in (1, 0) if (t, q) != (0, 0)]


def spot(c, block):
    o = block >> 2
    to = {"y": o >> 5, "x": (o >> 3) & 3, "z": (o >> 1) & 3}
    a1, a2, b = ORDERS[c]
    return ((to[b] * 2 + (o & 1)) * 4 + to[a2]) * 4 + to[a1]


def sweep(src, mag, decay, masks, x, visit, first_stage=True, second_stage=True):
    first, last = masks
    n = len(src)
    p = x + 1
    if first_stage:
        olds = [[s(c, p, 0) for c in range(3)] for s in src]
    befores = [None] * n
    for y in range(MY):
        if first_stage:
            stores = []
            for k in range(n):
                ex, ey, ez = olds[k]
                nx = [src[k](c, p, y + 1) for c in range(3)] if y + 1 < MY else None
                eyx, ezx = src[k](1, p + 1, y), src[k](2, p + 1, y)
                exz = jnp.where(last, 0.0, pltpu.roll(ex, MZ - 1, 1))
                eyz = jnp.where(last, 0.0, pltpu.roll(ey, MZ - 1, 1))
                h = mag[k]
                if y + 1 < MY:
                    gx = h[0, p + 1, y] + ((nx[2] - eyz) + (ey - ez))
                    gz = h[2, p + 1, y] + ((eyx - nx[0]) + (ex - ey))
                else:
                    gx = h[0, p + 1, y] + ((ey - ez) - eyz)
                    gz = h[2, p + 1, y] + (eyx + (ex - ey))
                gy = h[1, p + 1, y] + ((exz - ezx) + (ez - ex))
                olds[k] = nx
                stores.append((h, gx, gy, gz))
        if second_stage:
            keep = [decay[c, x, y] for c in range(3)]
            outs = []
            for k in range(n):
                h = mag[k]
                gx, gy, gz = (h[c, x + 1, y] for c in range(3))
                old = [src[k](c, x, y) for c in range(3)]
                gxz = jnp.where(first, 0.0, pltpu.roll(gx, 1, 1))
                gyz = jnp.where(first, 0.0, pltpu.roll(gy, 1, 1))
                gyx, gzx = h[1, x, y], h[2, x, y]
                if y > 0:
                    bx, bz = befores[k]
                    cx = (gz - gy) + (gyz - bz)
                    cz = (gy - gx) + (bx - gyx)
                else:
                    cx = (gz - gy) + gyz
                    cz = (gy - gx) - gyx
                cy = (gx - gz) + (gzx - gxz)
                new = [keep[c] * old[c] - 0.25 * v for c, v in enumerate((cx, cy, cz))]
                befores[k] = (gx, gz)
                outs.append((k, y, old, new))
        if first_stage:
            for h, gx, gy, gz in stores:
                h[0, p + 1, y] = gx
                h[1, p + 1, y] = gy
                h[2, p + 1, y] = gz
        if second_stage:
            for o in outs:
                visit(*o)


def kernel(ids, model, source, cotangent, fields, gradient,
           wish, gather, picked, arrived, asked_v, asked_s, raw, hist, cur, mag, decay, grad, layer,
           slots, landed, part, part_in, row_sum, row_in,
           s_raw, s_asked, s_wish, r_wish, s_a1, r_a1, s_a2, r_a2, s_b, r_b,
           s_gb, r_gb, s_g2, r_g2, s_g1, r_g1):
    me, at, core = place()
    pair = other_core(me, core, 1)
    started = []

    def go(copy):
        copy.start()
        started.append(copy)

    loads = [pltpu.make_async_copy(array, raw.at[k], s_raw.at[k]) for k, array in enumerate((source, cotangent))]
    for load in loads:
        load.start()
    barrier = pltpu.get_barrier_semaphore()
    near = neighbours(me, at, core)
    for other in near:
        pl.semaphore_signal(barrier, inc=1, device_id=(other,), device_id_type=MESH)
    for c, (a1, a2, b) in enumerate(ORDERS):
        for k in range(4):
            gather[c][0][at[a1], k] = model[pl.ds(c * 64 + k, MY, stride=4), :]
    pl.semaphore_wait(barrier, len(near))

    for k in FAR:
        for c, (a1, a2, b) in enumerate(ORDERS):
            own = gather[c][0].at[at[a1]]
            go(remote(own, own, s_a1.at[c, k], r_a1.at[c, k], shifted(me, at, a1, k)))

    def widen(j):
        for c, (a1, a2, b) in enumerate(ORDERS):
            at_j = (at[a1] + 4 - j) % 4
            slot = gather[c][0].at[at_j]
            if j:
                remote(slot, slot, s_a1.at[c, j], r_a1.at[c, j], pair).wait_recv()
            for k in FAR:
                go(remote(slot, gather[c][k].at[at_j], s_a2.at[c, k, j], r_a2.at[c, k, j], shifted(me, at, a2, k)))
    widen(0)

    lane = lax.broadcasted_iota(jnp.int32, (8, MZ), 1)

    def request(m, wanted):
        for i in range(16):
            block = ids[m, i]
            wanted = jnp.where(lane == (block >> 2), (m * 16 + i) * 4 + (block & 3), wanted)
        return wanted
    wanted = lax.fori_loop(0, 8, request, jnp.zeros((8, MZ), jnp.int32))
    wish[...] = wanted
    for c, (a1, a2, b) in enumerate(ORDERS):
        asked_v[c, 0, 0] = wanted
        for t, q in REACH:
            go(remote(wish, asked_v.at[c, t, q], s_wish.at[c, t, q], r_wish.at[c, t, q], column(me, at, core, b, t, q)))
    for j in (1, 3, 2):
        widen(j)
    for c in range(3):
        for t, q in REACH:
            remote(wish, asked_v.at[c, t, q], s_wish.at[c, t, q], r_wish.at[c, t, q], pair).wait_recv()
    loc = pltpu.make_async_copy(asked_v, asked_s, s_asked)
    loc.start()
    loc.wait()

    def place_of(b, side, row):
        return ((b * 2 + side) * 4 + row) * 4

    for k in (0, 1, 3, 2):
        for c, (a1, a2, b) in enumerate(ORDERS):
            row = (at[a2] + 4 - k) % 4
            if k:
                for j in range(4):
                    slot = gather[c][k].at[(at[a1] + 4 - j) % 4]
                    remote(slot, slot, s_a2.at[c, k, j], r_a2.at[c, k, j], pair).wait_recv()
            base = me + (row - at[a2]) * STRIDE[a2] - at[a1] * STRIDE[a1]
            spots = place_of(at[b], core, row)
            for t, q in REACH + [(0, 0)]:
                for i in range(4):
                    block = gather[c][k][i, asked_s[c, (4 - t) % 4, q, 0, base + i * STRIDE[a1]] & 3]
                    if (t, q) == (0, 0):
                        arrived[c, spots + i] = block
                    else:
                        picked[c, t, q, row, i] = block
                if (t, q) != (0, 0):
                    go(remote(picked.at[c, t, q, row], arrived.at[c, pl.ds(spots, 4)],
                              s_b.at[c, k, t, q], r_b.at[c, k, t, q], column(me, at, core, b, t, q)))

    zero = jnp.zeros((8, MZ), jnp.float32)

    def clear(i, carry):
        for c in range(3):
            for k in range(2):
                mag[k, c, i // MY, i % MY] = zero
        return carry
    lax.fori_loop(0, (MX + 1) * MY, clear, 0)

    def clear_grad(i, carry):
        for c in range(3):
            grad[c, i // MY, i % MY] = zero
            decay[c, i // MY, i % MY] = zero
        return carry
    lax.fori_loop(0, MX * MY, clear_grad, 0)

    for y in range(MY):
        for k in range(2):
            for c in (1, 2):
                cur[k, c, MX, y] = zero
    for load in loads:
        load.wait()

    def stage(i, carry):
        for y in range(MY):
            for k in range(2):
                cur[k, i // MX, i % MX, y] = raw[k, pl.ds(i * MY + y, 8, stride=3 * MX * MY), :]
        return carry
    lax.fori_loop(0, 3 * MX, stage, 0)

    masks = (lane == 0, lane == MZ - 1)
    state = [lambda c, x, y, k=k: cur[k, c, x, y] for k in range(2)]
    mags = [mag.at[k] for k in range(2)]

    def early(n, carry):
        def plane(x, carry, **which):
            def visit(k, y, old, new):
                for c in range(3):
                    hist[k, n, c, x, y] = old[c]
                    cur[k, c, x, y] = new[c]
            sweep(state, mags, decay, masks, x, visit, **which)
            return carry
        plane(-1, 0, second_stage=False)
        lax.fori_loop(0, MX - 1, plane, carry)
        plane(MX - 1, 0, first_stage=False)
        return carry

    lax.fori_loop(0, 1, early, 0)

    for k in range(4):
        for c, (a1, a2, b) in enumerate(ORDERS):
            row = (at[a2] + 4 - k) % 4
            for t, q in REACH:
                slot = arrived.at[c, pl.ds(place_of((at[b] + 4 - t) % 4, core + (1 - 2 * core) * q, row), 4)]
                remote(slot, slot, s_b.at[c, k, t, q], r_b.at[c, k, t, q], pair).wait_recv()

    flat_decay = decay.reshape(3 * MX * MY * 8, MZ)
    flat_grad = grad.reshape(3 * MX * MY * 8, MZ)

    def blend(m, carry):
        for x in range(MX):
            f = ids[m, 2 * MX + x].astype(jnp.float32) * 0.125
            for c in range(3):
                close = arrived[c, spot(c, ids[m, x])]
                far = arrived[c, spot(c, ids[m, MX + x])]
                mixed = 1.0 - 0.5 * (f * close + (1.0 - f) * far)
                flat_decay[pl.ds((c * MX + x) * (MY * 8) + m, MY, stride=8), :] = mixed
        return carry
    lax.fori_loop(0, 8, blend, 0)

    def damp(i, carry):
        c, x = i // MX, i % MX
        for y in range(MY):
            for k in range(2):
                cur[k, c, x, y] = decay[c, x, y] * hist[k, 0, c, x, y] + cur[k, c, x, y]
        return carry
    lax.fori_loop(0, 3 * MX, damp, 0)
    lax.fori_loop(1, HALF, early, 0)

    def late(n, carry):
        def plane(x, carry, **which):
            terms = {}

            def visit(k, y, old, new):
                terms[k] = [old[c] * hist[1 - k, STEPS - 1 - n, c, x, y] for c in range(3)]
                for c in range(3):
                    if k == 1:
                        grad[c, x, y] = grad[c, x, y] + (terms[0][c] + terms[1][c])
                    cur[k, c, x, y] = new[c]
            sweep(state, mags, decay, masks, x, visit, **which)
            return carry
        plane(-1, 0, second_stage=False)
        lax.fori_loop(0, MX - 1, plane, carry)
        plane(MX - 1, 0, first_stage=False)
        return carry
    lax.fori_loop(HALF, STEPS - 1, late, 0)

    def unstage(i, carry):
        c, x = i // MX, i % MX
        for y in range(MY):
            grad[c, x, y] = grad[c, x, y] + (cur[0, c, x, y] * hist[1, 0, c, x, y] + cur[1, c, x, y] * hist[0, 0, c, x, y])
        for m in range(8):
            layer[i * 8 + m] = flat_grad[pl.ds(i * (MY * 8) + m, MY, stride=8), :]
        return carry
    lax.fori_loop(0, 3 * MX, unstage, 0)

    def landing(c, t, q, row, k, b, device):
        spots = place_of((at[b] + t) % 4, core + (1 - 2 * core) * q, row)
        return remote(slots.at[c, pl.ds(spots, 4)], landed.at[c, t, q, row], s_gb.at[c, k, t, q], r_gb.at[c, k, t, q], device)

    def rowwise(c, k, j, i, a2):
        return remote(part.at[c, k, i], part_in.at[c, k, i], s_g2.at[c, k, j], r_g2.at[c, k, j], shifted(me, at, a2, k))

    for k in (2, 1, 3, 0):
        for c, (a1, a2, b) in enumerate(ORDERS):
            row = (at[a2] + k) % 4
            for t, q in REACH + [(0, 0)]:
                side = core + (1 - 2 * core) * q
                to = (at[b] + t) % 4
                base = to * STRIDE[b] + side + row * STRIDE[a2]
                for i in range(4):
                    e = asked_s[c, 0, 0, 0, base + i * STRIDE[a1]] >> 2
                    x = e & 7
                    f = ids[e >> 4, 2 * MX + x].astype(jnp.float32) * 0.125
                    scale = jnp.where((e & 8) == 0, f, 1.0 - f) * -0.5
                    slots[c, place_of(to, side, row) + i] = scale * layer[(c * MX + x) * 8 + (e >> 4)]
                if (t, q) != (0, 0):
                    go(landing(c, t, q, row, k, b, column(me, at, core, b, t, q)))

    def final(carry):
        def plane(x, carry, **which):
            def visit(k, y, old, new):
                for c in range(3):
                    fields[pl.ds((c * MX + x) * MY + y, 8, stride=3 * MX * MY), :] = new[c]
            sweep(state[:1], mags[:1], decay, masks, x, visit, **which)
            return carry
        plane(-1, 0, second_stage=False)
        lax.fori_loop(0, MX - 1, plane, carry)
        plane(MX - 1, 0, first_stage=False)
        return carry
    final(0)

    for k in (2, 1, 3, 0):
        for c, (a1, a2, b) in enumerate(ORDERS):
            row = (at[a2] + k) % 4
            for t, q in REACH:
                landing(c, t, q, row, k, b, pair).wait_recv()
            base = me + (row - at[a2]) * STRIDE[a2] - at[a1] * STRIDE[a1]
            for j in (2, 1, 3, 0):
                i = (at[a1] + j) % 4
                who = asked_s[c, 0, 0, 0, base + i * STRIDE[a1]] & 3
                own = slots[c, place_of(at[b], core, row) + i]
                total = [jnp.where(who == n, own, 0.0) for n in range(4)]
                for t, q in REACH:
                    who = asked_s[c, t, q, 0, base + i * STRIDE[a1]] & 3
                    term = landed[c, t, q, row, i]
                    total = [v + jnp.where(who == n, term, 0.0) for n, v in enumerate(total)]
                for n in range(4):
                    part[c, k, i, n] = total[n]
                if k:
                    go(rowwise(c, k, j, i, a2))
    for j in (2, 1, 3, 0):
        for c, (a1, a2, b) in enumerate(ORDERS):
            i = (at[a1] + j) % 4
            for k in FAR:
                rowwise(c, k, j, i, a2).wait_recv()
            for n in range(4):
                row_sum[c, j, n] = (part[c, 0, i, n] + part_in[c, 1, i, n]) + (part_in[c, 2, i, n] + part_in[c, 3, i, n])
            if j:
                go(remote(row_sum.at[c, j], row_in.at[c, j], s_g1.at[c, j], r_g1.at[c, j], shifted(me, at, a1, j)))
    for c in range(3):
        for j in FAR:
            remote(row_sum.at[c, j], row_in.at[c, j], s_g1.at[c, j], r_g1.at[c, j], pair).wait_recv()
        for n in range(4):
            gradient[pl.ds(c * 64 + n, MY, stride=4), :] = (row_sum[c, 0, n] + row_in[c, 1, n]) + (row_in[c, 2, n] + row_in[c, 3, n])
    for copy in started:
        copy.wait_send()


def run(ids, model, source, cotangent):
    vmem = pl.BlockSpec(memory_space=pltpu.VMEM)
    smem = pl.BlockSpec(memory_space=pltpu.SMEM)
    anywhere = pl.BlockSpec(memory_space=pl.ANY)
    f32, i32 = jnp.float32, jnp.int32
    dma = pltpu.SemaphoreType.DMA
    rows = 8 * 3 * MX * MY
    return pl.pallas_call(
        kernel,
        out_shape=(jax.ShapeDtypeStruct((rows, MZ), f32), jax.ShapeDtypeStruct((192, MZ), f32)),
        in_specs=[smem, vmem, anywhere, anywhere],
        out_specs=(vmem, vmem),
        scratch_shapes=[
            pltpu.VMEM((8, MZ), i32),
            [[pltpu.VMEM((4, 4, MY, MZ), f32) for k in range(4)] for c in range(3)],
            pltpu.VMEM((3, 4, 2, 4, 4, MY, MZ), f32),
            pltpu.VMEM((3, 128, MY, MZ), f32),
            pltpu.VMEM((3, 4, 2, 8, MZ), i32),
            pltpu.SMEM((3, 4, 2, 8, MZ), i32),
            pltpu.VMEM((2, rows, MZ), f32),
            pltpu.VMEM((2, HALF, 3, MX, MY, 8, MZ), f32),
            pltpu.VMEM((2, 3, MX + 1, MY, 8, MZ), f32),
            pltpu.VMEM((2, 3, MX + 1, MY, 8, MZ), f32),
            pltpu.VMEM((3, MX, MY, 8, MZ), f32),
            pltpu.VMEM((3, MX, MY, 8, MZ), f32),
            pltpu.VMEM((3 * MX * 8, MY, MZ), f32),
            pltpu.VMEM((3, 128, MY, MZ), f32),
            pltpu.VMEM((3, 4, 2, 4, 4, MY, MZ), f32),
            pltpu.VMEM((3, 4, 4, 4, MY, MZ), f32),
            pltpu.VMEM((3, 4, 4, 4, MY, MZ), f32),
            pltpu.VMEM((3, 4, 4, MY, MZ), f32),
            pltpu.VMEM((3, 4, 4, MY, MZ), f32),
            dma((2,)), dma,
            dma((3, 4, 2)), dma((3, 4, 2)),
            dma((3, 4)), dma((3, 4)),
            dma((3, 4, 4)), dma((3, 4, 4)),
            dma((3, 4, 4, 2)), dma((3, 4, 4, 2)),
            dma((3, 4, 4, 2)), dma((3, 4, 4, 2)),
            dma((3, 4, 4)), dma((3, 4, 4)),
            dma((3, 4)), dma((3, 4)),
        ],
        compiler_params=pltpu.CompilerParams(collective_id=0, has_side_effects=True, vmem_limit_bytes=51 * 2**20),
    )(ids, model, source, cotangent)


def local(conductivity, block_ids, weights, source, cotangent):
    blocks = conductivity.shape[0]
    model = conductivity.reshape(blocks, 3, MY, MZ).transpose(1, 2, 0, 3).reshape(3 * MY * blocks, MZ)
    fields, gradient = run(jnp.concatenate([block_ids, weights], axis=1), model, source.reshape(-1, MZ), cotangent.reshape(-1, MZ))
    gradient = gradient.reshape(3, MY, blocks, MZ).transpose(2, 0, 1, 3)
    return fields.reshape(source.shape), gradient.reshape(conductivity.shape)


def solution(mesh):
    rows = P("dev")
    return jax.shard_map(
        local, mesh=mesh, in_specs=(rows,) * 5, out_specs=(rows, rows), check_vma=False
    )
```
